1024 devices in a mesh: lon: 64 (over y, z_hi, x), lat: 16 (over z_lo, core).
Axes of the slice: x: 4, y: 4, z: 32 (z_hi: 4, z_lo: 8; z = z_hi * 8 + z_lo), core: 2. Of those that a mesh axis runs over, the one named last changes fastest.
Arguments:
- tracers: float32 [2, 8, 768, 8192], P(None, None, 'lat', 'lon'), may hold values from -6 to 6
- east_courant: float32 [8, 768, 8192], P(None, 'lat', 'lon'), may hold values from -0.25 to 0.25
- north_courant: float32 [8, 768, 8192], P(None, 'lat', 'lon'), may hold values from -0.25 to 0.25
- diffusivity: float32 [8, 768, 8192], P(None, 'lat', 'lon'), may hold values from 0.01 to 0.12
- wet_levels: int32 [768, 8192], P('lat', 'lon'), may hold values from 0 to 8
Outputs:
- advected: float32 [2, 8, 768, 8192], P(None, None, 'lat', 'lon')
The draws below stay inside these ranges and needn't reach their ends.
All inputs are finite; a program needn't handle non-finite values.
Results may differ from the reference program's by a relative error of at most 0.0003.
Values sent between devices are 32-bit elements; how exact they have to be, the bound alone decides.
A program may use at most 32 MiB of HBM per device.

```python
import math
import jax
import jax.numpy as jnp

LEV = 8
STEPS = 3
NLON = 8192
NLAT = 768


def set_ends(entries, key, least, largest):
    dims = entries.shape
    index_at = [jax.random.randint(jax.random.fold_in(key, axis), (), 0, dims[axis]) for axis in range(len(dims))]
    entries = entries.at[tuple(index_at)].set(least)
    longest = dims.index(max(dims))
    index_at[longest] = (index_at[longest] + 1) % dims[longest]
    return entries.at[tuple(index_at)].set(largest)


def steps_of(own_key, shape, pieces, least, largest):
    def one(axis_at, shards_of):
        draws = jax.random.uniform(jax.random.fold_in(jax.random.fold_in(own_key, 6), axis_at), (shards_of,), jnp.float32, least / len(pieces), largest / len(pieces))
        return jnp.repeat(jnp.exp(draws), shape[axis_at] // shards_of).reshape((-1,) + (1,) * (len(shape) - axis_at - 1))

    loudness = one(*pieces[0])
    for cut in pieces[1:]:
        loudness = loudness * one(*cut)
    return loudness


def normal_values(own_key, extent, spread, limit, split=(), kind=jnp.bfloat16):
    level = steps_of(own_key, extent, split, -0.22, 0.18) if split else 1.0
    result = jax.random.normal(own_key, extent, jnp.float32) * spread * level
    return jnp.minimum(jnp.maximum(result, -limit), limit).astype(kind)


def setup_inputs(seed: int = 0) -> dict:
    splits = jax.random.split(jax.random.key(seed), 6)
    tracers = normal_values(splits[0], (2, LEV, NLAT, NLON), 1.0, 6.0, ((2, 16), (3, 64)), jnp.float32)
    east_courant = jnp.clip(jax.random.uniform(splits[1], (LEV, NLAT, NLON), jnp.float32, -0.25, 0.25) * steps_of(splits[1], (LEV, NLAT, NLON), ((1, 16), (2, 64)), -0.4, 0.0), -0.25, 0.25)
    north_courant = jnp.clip(jax.random.uniform(splits[2], (LEV, NLAT, NLON), jnp.float32, -0.25, 0.25) * steps_of(splits[2], (LEV, NLAT, NLON), ((1, 16), (2, 64)), -0.4, 0.0), -0.25, 0.25)
    diffusivity = jnp.clip(jnp.exp(math.log(0.12) - 2.4849066 * jax.random.uniform(splits[3], (LEV, NLAT, NLON), jnp.float32) ** steps_of(splits[3], (LEV, NLAT, NLON), ((1, 16), (2, 64)), -0.2, 0.2)), 0.01, 0.12)
    wet_levels = set_ends(jax.random.randint(splits[4], (NLAT, NLON), 0, LEV + 1), jax.random.fold_in(splits[4], 1), 0, LEV).astype(jnp.int32)
    return dict(tracers=tracers, east_courant=east_courant, north_courant=north_courant, diffusivity=diffusivity, wet_levels=wet_levels)


def minmod(first, second):
    return 0.5 * (jnp.sign(first) + jnp.sign(second)) * jnp.minimum(jnp.abs(first), jnp.abs(second))


def face_flux(behind, left_cell, right_cell, beyond, courant, face_kappa, face_mask):
    difference = right_cell - left_cell
    forward = courant > 0
    upwind = jnp.where(forward, left_cell, right_cell)
    upslope = jnp.where(forward, left_cell - behind, beyond - right_cell)
    magnitude = jnp.abs(courant)
    limited = minmod(difference, upslope)
    return (courant * upwind + 0.5 * magnitude * (1.0 - magnitude) * limited - face_kappa * difference) * face_mask


def reference(tracers, east_courant, north_courant, diffusivity, wet_levels):
    layers = jnp.arange(LEV, dtype=jnp.int32)[:, None, None]
    wetness = (layers < wet_levels[None]).astype(jnp.float32)
    east_kappa = 0.5 * (diffusivity + jnp.roll(diffusivity, -1, 2))
    east_mask = wetness * jnp.roll(wetness, -1, 2)
    fold_speed = 0.5 * (north_courant[:, -1] - north_courant[:, -1, ::-1])
    empty_row = jnp.zeros((LEV, 1, NLON), jnp.float32)
    north_speed = jnp.concatenate([empty_row, north_courant[:, :NLAT - 1], fold_speed[:, None]], 1)
    kappa_rows = jnp.concatenate([empty_row, diffusivity, diffusivity[:, -1:, ::-1]], 1)
    wet_rows = jnp.concatenate([empty_row, wetness, wetness[:, -1:, ::-1]], 1)
    north_kappa = 0.5 * (kappa_rows[:, :-1] + kappa_rows[:, 1:])
    north_mask = wet_rows[:, :-1] * wet_rows[:, 1:]
    face_count = NLAT + 1
    current = tracers
    for repeat in range(STEPS):
        east_flux = face_flux(jnp.roll(current, 1, 3), current, jnp.roll(current, -1, 3), jnp.roll(current, -2, 3), east_courant, east_kappa, east_mask)
        extended = jnp.concatenate([jnp.zeros((2, LEV, 2, NLON), jnp.float32), current, current[:, :, -1:, ::-1], current[:, :, -2:-1, ::-1]], 2)
        north_flux = face_flux(extended[:, :, 0:face_count], extended[:, :, 1:face_count + 1], extended[:, :, 2:face_count + 2], extended[:, :, 3:face_count + 3], north_speed, north_kappa, north_mask)
        current = current - (east_flux - jnp.roll(east_flux, 1, 3)) - (north_flux[:, :, 1:] - north_flux[:, :, :-1])
    return current
```

```python
import functools

import jax
import jax.numpy as jnp
from jax import lax
from jax.experimental import pallas as pl
from jax.experimental.pallas import tpu as pltpu
from jax.sharding import PartitionSpec as P

MESH = pl.DeviceIdType.MESH
LEVELS, ROWS, COLS = 8, 48, 128
PAD = 8
SPAN = ROWS + 2 * PAD
REACH = 6
UNROLL = 4
T0, T1, EAST, NORTH, KAPPA, WET = range(6)
SLOTS = ((6, 6), (6, 12), (5, 17), (4, 21), (5, 26), (5, 31))


def roll(value, shift):
    return pltpu.roll(value, shift % COLS, 1)


def lane_index():
    return lax.broadcasted_iota(jnp.int32, (LEVELS, COLS), 1)


def reverse(value):
    return jnp.take_along_axis(value, COLS - 1 - lane_index(), axis=1, mode="promise_in_bounds")


def face(speed, kappa_sum, mask):
    speed = speed * mask
    magnitude = jnp.abs(speed)
    return (
        speed,
        jnp.minimum(speed, 0.0) - 0.5 * kappa_sum * mask,
        0.5 * magnitude * (1.0 - magnitude),
    )


def flux(cell, before, here, after, coef):
    speed, drift, limit = coef
    upslope = jnp.where(speed > 0, before, after)
    limited = jnp.minimum(jnp.maximum(upslope, jnp.minimum(here, 0.0)), jnp.maximum(here, 0.0))
    return speed * cell + drift * here + limit * limited


def coefficients(row, east, north, kappa, wet, out, first=0):
    here, above = kappa(row), kappa(row + 1)
    wet_here, wet_above = wet(row), wet(row + 1)
    along = face(east(row), here + roll(here, -1), wet_here * roll(wet_here, -1))
    across = face(north(row), here + above, wet_here * wet_above)
    for number, value in enumerate(along + across):
        out[row, number] = value


def advance(source, coef, start, count, store, width=UNROLL):
    def north_flux(row, tracer, cell, diffs):
        return flux(cell, *diffs, tuple(coef[row, 3 + k] for k in range(3)))

    def first_flux(tracer):
        cells = [source(start - 2 + k, tracer) for k in range(4)]
        diffs = [cells[k + 1] - cells[k] for k in range(3)]
        return north_flux(start - 1, tracer, cells[1], diffs)

    def body(number, below):
        base = start + number * width
        below = list(below)
        for tracer in range(2):
            cells = [source(base - 1 + k, tracer) for k in range(width + 3)]
            diffs = [cells[k + 1] - cells[k] for k in range(width + 2)]
            for k in range(width):
                row = base + k
                cell = cells[k + 1]
                here = roll(cell, -1) - cell
                along = flux(
                    cell, roll(here, 1), here, roll(here, -1), tuple(coef[row, i] for i in range(3))
                )
                across = north_flux(row, tracer, cell, diffs[k : k + 3])
                store(row, tracer, cell - (along - roll(along, 1)) - (across - below[tracer]))
                below[tracer] = across
        return tuple(below)

    below = (first_flux(0), first_flux(1))
    if count == width:
        body(0, below)
    else:
        lax.fori_loop(0, count // width, body, below)


def kernel(
    nlon, nlat,
    tracers_hbm, east_hbm, north_hbm, kappa_hbm, levels_hbm, out_ref,
    tracers_in, east_in, north_in, kappa_in, levels,
    cells, wet, to_east, to_west, from_west, from_east, strip,
    main_coef, strip_coef, main_1, main_2, main_3, strip_1, strip_2,
    load_sem, send_sem, recv_sem,
):
    lon, lat = lax.axis_index("lon"), lax.axis_index("lat")
    at_top, at_bottom = lat == nlat - 1, lat == 0
    below_top, above_bottom = jnp.logical_not(at_top), jnp.logical_not(at_bottom)
    east_lon, west_lon = lax.rem(lon + 1, nlon), lax.rem(lon + nlon - 1, nlon)
    fold_lon, fold_east, fold_west = nlon - 1 - lon, nlon - 1 - east_lon, nlon - 1 - west_lon
    east_is_self = jnp.logical_and(at_top, fold_east == lon)
    west_is_self = jnp.logical_and(at_top, fold_west == lon)
    lane = lane_index()

    north_lat = jnp.where(at_top, lat, lat + 1)
    south_lat = jnp.where(at_bottom, lat, lat - 1)
    north = (jnp.where(at_top, fold_lon, lon), north_lat)
    north_east = (jnp.where(at_top, fold_east, east_lon), north_lat)
    north_west = (jnp.where(at_top, fold_west, west_lon), north_lat)
    south, south_east, south_west = (lon, south_lat), (east_lon, south_lat), (west_lon, south_lat)

    partners = (
        ((east_lon, lat), None),
        ((west_lon, lat), None),
        (north, None),
        (north_east, jnp.logical_not(east_is_self)),
        (north_west, jnp.logical_not(west_is_self)),
        (south, above_bottom),
        (south_east, above_bottom),
        (south_west, above_bottom),
    )

    def under(condition, action):
        if condition is None:
            action()
        else:
            pl.when(condition)(action)

    barrier = pltpu.get_barrier_semaphore()
    for device, condition in partners:
        under(
            condition,
            lambda device=device: pl.semaphore_signal(
                barrier, 1, device_id=device, device_id_type=MESH
            ),
        )

    loads = [
        pltpu.make_async_copy(source, target, load_sem.at[number])
        for number, (source, target) in enumerate(
            (
                (levels_hbm, levels.at[pl.ds(PAD, ROWS)]),
                (tracers_hbm, tracers_in),
                (east_hbm, east_in),
                (north_hbm, north_in),
                (kappa_hbm, kappa_in),
            )
        )
    ]
    for copy in loads:
        copy.start()

    @pl.when(at_bottom)
    def _():
        zero = jnp.zeros((LEVELS, COLS), jnp.float32)
        levels[pl.ds(0, PAD)] = jnp.zeros((PAD, COLS), jnp.int32)
        for row in range(PAD - REACH, PAD):
            for number in range(5):
                cells[row, number] = zero
        for number in range(2):
            from_west[number] = zero
            from_east[number] = zero

    for copy in loads:
        copy.wait()

    depth = lax.broadcasted_iota(jnp.int32, (LEVELS, COLS), 0)

    def wet_row(row):
        return (depth < levels[pl.ds(row, 1)]).astype(jnp.float32)

    def gather(number, carry):
        eastern = jnp.zeros((LEVELS, COLS), jnp.float32)
        western = jnp.zeros((LEVELS, COLS), jnp.float32)
        for group in range(4):
            row = number * 4 + group
            values = [
                tracers_in[pl.ds(row, LEVELS, stride=ROWS)],
                tracers_in[pl.ds(row + LEVELS * ROWS, LEVELS, stride=ROWS)],
                east_in[pl.ds(row, LEVELS, stride=ROWS)],
                north_in[pl.ds(row, LEVELS, stride=ROWS)],
                kappa_in[pl.ds(row, LEVELS, stride=ROWS)],
                wet_row(row + PAD),
            ]
            for which in range(5):
                cells[row + PAD, which] = values[which]
            wet[row + PAD] = values[WET]
            for which, (width, end) in enumerate(SLOTS):
                last = 32 * group + end
                inside = jnp.logical_and(lane >= last - width, lane < last)
                eastern = jnp.where(inside, roll(values[which], last), eastern)
                start = 32 * group + 32 - end
                inside = jnp.logical_and(lane >= start, lane < start + width)
                western = jnp.where(inside, roll(values[which], start), western)
        to_east[number] = eastern
        to_west[number] = western
        return carry

    lax.fori_loop(0, ROWS // 4, gather, 0)

    count = 3 + sum(
        condition.astype(jnp.int32) for _, condition in partners if condition is not None
    )
    pl.semaphore_wait(barrier, count)

    own = pl.ds(2, ROWS // 4)
    low, high = pl.ds(0, 2), pl.ds(2 + ROWS // 4, 2)
    top_groups = pl.ds(ROWS // 4 - 2, 2)
    low_rows, high_rows = pl.ds(PAD - REACH, REACH), pl.ds(PAD + ROWS, REACH)
    first_rows, last_rows = pl.ds(PAD, REACH), pl.ds(PAD + ROWS - REACH, REACH)

    def remote(source, target, send, receive, device):
        return pltpu.make_async_remote_copy(
            src_ref=source,
            dst_ref=target,
            send_sem=send_sem.at[send],
            recv_sem=recv_sem.at[receive],
            device_id=device,
            device_id_type=MESH,
        )

    remote(to_east, from_west.at[own], 0, 0, (east_lon, lat)).start()
    remote(to_west, from_east.at[own], 1, 1, (west_lon, lat)).start()

    @pl.when(at_top)
    def _():
        remote(cells.at[last_rows], cells.at[high_rows], 6, 7, north).start()
        remote(levels.at[pl.ds(ROWS, 8)], levels.at[pl.ds(PAD + ROWS, 8)], 8, 9, north).start()

        @pl.when(jnp.logical_not(east_is_self))
        def _():
            remote(to_east.at[top_groups], from_east.at[high], 2, 5, north_east).start()

        @pl.when(jnp.logical_not(west_is_self))
        def _():
            remote(to_west.at[top_groups], from_west.at[high], 3, 4, north_west).start()

        @pl.when(east_is_self)
        def _():
            from_east[high] = to_east[top_groups]

        @pl.when(west_is_self)
        def _():
            from_west[high] = to_west[top_groups]

    @pl.when(below_top)
    def _():
        remote(to_east.at[top_groups], from_west.at[low], 2, 2, north_east).start()
        remote(to_west.at[top_groups], from_east.at[low], 3, 3, north_west).start()

    @pl.when(above_bottom)
    def _():
        remote(to_east.at[low], from_west.at[high], 4, 4, south_east).start()
        remote(to_west.at[low], from_east.at[high], 5, 5, south_west).start()
        remote(levels.at[pl.ds(PAD, 8)], levels.at[pl.ds(PAD + ROWS, 8)], 9, 9, south).start()
        remote(cells.at[first_rows], cells.at[high_rows], 7, 7, south).start()

    @pl.when(below_top)
    def _():
        remote(levels.at[pl.ds(ROWS, 8)], levels.at[pl.ds(0, 8)], 8, 8, north).start()
        remote(cells.at[last_rows], cells.at[low_rows], 6, 6, north).start()


    def folded(value):
        return jnp.where(lane < COLS // 2, roll(value, REACH), roll(value, -REACH))

    def strip_own(number, carry):
        for k in range(2):
            row = PAD + 2 * number + k
            for which in range(5):
                strip[row, which] = folded(cells[row, which])
            strip[row, WET] = folded(wet[row])
        return carry

    lax.fori_loop(0, ROWS // 2, strip_own, 0)

    main_parts = (
        lambda row: cells[row, EAST],
        lambda row: cells[row, NORTH],
        lambda row: cells[row, KAPPA],
        lambda row: wet[row],
    )
    strip_parts = tuple(
        lambda row, which=which: strip[row, which] for which in (EAST, NORTH, KAPPA, WET)
    )

    def main_coefficients(number, carry):
        for k in range(2):
            coefficients(PAD + 2 * number + k, *main_parts, main_coef)
        return carry

    lax.fori_loop(0, ROWS // 2 - 1, main_coefficients, 0)

    def keep(target):
        def store(row, tracer, value):
            target[row, tracer] = value

        return store

    def reading(source):
        return lambda row, tracer: source[row, tracer]

    stages = (reading(cells), reading(main_1), reading(main_2))
    targets = (keep(main_1), keep(main_2), keep(main_3))
    for step in range(3):
        margin = 2 * (step + 1)
        advance(stages[step], main_coef, PAD + margin, ROWS - 2 * margin, targets[step])


    def arrival(slot, target):
        remote(target, target, slot, slot, (lon, lat)).wait_recv()

    def departure(slot, source):
        remote(source, source, slot, slot, (lon, lat)).wait_send()

    arrival(7, cells.at[high_rows])
    arrival(9, levels.at[pl.ds(PAD + ROWS, 8)])
    pl.when(jnp.logical_not(west_is_self))(lambda: arrival(4, from_west.at[high]))
    pl.when(jnp.logical_not(east_is_self))(lambda: arrival(5, from_east.at[high]))

    @pl.when(above_bottom)
    def _():
        arrival(6, cells.at[low_rows])
        arrival(8, levels.at[pl.ds(0, 8)])
        arrival(2, from_west.at[low])
        arrival(3, from_east.at[low])

    arrival(0, from_west.at[own])
    arrival(1, from_east.at[own])

    departure(0, to_east)
    departure(1, to_west)
    pl.when(jnp.logical_not(east_is_self))(lambda: departure(2, to_east.at[top_groups]))
    pl.when(jnp.logical_not(west_is_self))(lambda: departure(3, to_west.at[top_groups]))
    departure(6, cells.at[last_rows])
    departure(8, levels.at[pl.ds(ROWS, 8)])

    @pl.when(above_bottom)
    def _():
        departure(4, to_east.at[low])
        departure(5, to_west.at[low])
        departure(7, cells.at[first_rows])
        departure(9, levels.at[pl.ds(PAD, 8)])

    north_start = PAD + ROWS
    raw_start = jnp.where(at_top, north_start + 2, north_start)
    for k in range(REACH):
        wet[PAD - REACH + k] = wet_row(PAD - REACH + k)
        wet[north_start + k] = wet_row(raw_start + k)

    @pl.when(at_top)
    def _():
        for side in (from_west, from_east):
            lower, upper = side[2 + ROWS // 4], side[3 + ROWS // 4]
            side[2 + ROWS // 4], side[3 + ROWS // 4] = reverse(upper), reverse(lower)

        def swap(k, carry):
            one, other = north_start + k, north_start + REACH - 1 - k
            for which in range(5):
                near, far = cells[one, which], cells[other, which]
                cells[one, which], cells[other, which] = reverse(far), reverse(near)
            near, far = wet[one], wet[other]
            wet[one], wet[other] = reverse(far), reverse(near)
            return carry

        lax.fori_loop(0, REACH // 2, swap, 0)

    def edged(row_group, group, which, value):
        end = SLOTS[which][1]
        left = roll(from_west[row_group], REACH - 32 * group - end)
        right = roll(from_east[row_group], COLS - REACH - 32 - 32 * group + end)
        return jnp.where(lane < REACH, left, jnp.where(lane >= COLS - REACH, right, value))

    def strip_ghost(row_group, groups):
        for group in groups:
            row = 4 * row_group + group
            for which in range(5):
                strip[row, which] = edged(row_group, group, which, folded(cells[row, which]))
            strip[row, WET] = edged(row_group, group, WET, folded(wet[row]))

    strip_ghost(0, (2, 3))
    strip_ghost(1, range(4))
    strip_ghost(2 + ROWS // 4, range(4))
    strip_ghost(3 + ROWS // 4, (0, 1))

    def strip_edges(number, carry):
        row_group = number + 2
        for group in range(4):
            row = 4 * row_group + group
            for which in range(6):
                strip[row, which] = edged(row_group, group, which, strip[row, which])
        return carry

    lax.fori_loop(0, ROWS // 4, strip_edges, 0)

    @pl.when(at_top)
    def _():
        last = north_start - 1
        for part in (cells, strip):
            part[last, NORTH] = 0.5 * (part[last, NORTH] - part[north_start, NORTH])
            for k in range(4):
                row = north_start + k
                part[row, NORTH] = -part[row + 1, NORTH]
                part[row, EAST] = -roll(part[row, EAST], -1)

    for row in (3, 4, 5, 6, 7, 54, 55, 56, 57, 58, 59):
        coefficients(row, *main_parts, main_coef)

    for step in range(3):
        reach = REACH - 2 * (step + 1)
        advance(stages[step], main_coef, PAD - reach, REACH, targets[step], REACH)
        advance(stages[step], main_coef, PAD + ROWS - 2 * (step + 1), REACH, targets[step], REACH)

    def strip_coefficients(number, carry):
        for k in range(3):
            coefficients(3 + 3 * number + k, *strip_parts, strip_coef)
        return carry

    lax.fori_loop(0, 19, strip_coefficients, 0)

    advance(reading(strip), strip_coef, PAD - 4, ROWS + 8, keep(strip_1))
    advance(reading(strip_1), strip_coef, PAD - 2, ROWS + 4, keep(strip_2))

    def finish(row, tracer, value):
        merged = jnp.where(
            lane < REACH,
            roll(value, -REACH),
            jnp.where(lane >= COLS - REACH, roll(value, REACH), main_3[row, tracer]),
        )
        out_ref[pl.ds(tracer * LEVELS * ROWS + row - PAD, LEVELS, stride=ROWS)] = merged

    advance(reading(strip_2), strip_coef, PAD, ROWS, finish)


def per_device(nlon, nlat, tracers, east_courant, north_courant, diffusivity, wet_levels):
    flat = LEVELS * ROWS
    f32 = jnp.float32
    vreg = (LEVELS, COLS)
    result = pl.pallas_call(
        functools.partial(kernel, nlon, nlat),
        out_shape=jax.ShapeDtypeStruct((2 * flat, COLS), f32),
        in_specs=[pl.BlockSpec(memory_space=pltpu.HBM)] * 5,
        out_specs=pl.BlockSpec(memory_space=pltpu.VMEM),
        scratch_shapes=[
            pltpu.VMEM((2 * flat, COLS), f32),
            pltpu.VMEM((flat, COLS), f32),
            pltpu.VMEM((flat, COLS), f32),
            pltpu.VMEM((flat, COLS), f32),
            pltpu.VMEM((SPAN, COLS), jnp.int32),
            pltpu.VMEM((SPAN, 5) + vreg, f32),
            pltpu.VMEM((SPAN,) + vreg, f32),
            pltpu.VMEM((ROWS // 4,) + vreg, f32),
            pltpu.VMEM((ROWS // 4,) + vreg, f32),
            pltpu.VMEM((SPAN // 4,) + vreg, f32),
            pltpu.VMEM((SPAN // 4,) + vreg, f32),
            pltpu.VMEM((SPAN, 6) + vreg, f32),
            pltpu.VMEM((SPAN, 6) + vreg, f32),
            pltpu.VMEM((SPAN, 6) + vreg, f32),
            pltpu.VMEM((SPAN, 2) + vreg, f32),
            pltpu.VMEM((SPAN, 2) + vreg, f32),
            pltpu.VMEM((SPAN, 2) + vreg, f32),
            pltpu.VMEM((SPAN, 2) + vreg, f32),
            pltpu.VMEM((SPAN, 2) + vreg, f32),
            pltpu.SemaphoreType.DMA((5,)),
            pltpu.SemaphoreType.DMA((10,)),
            pltpu.SemaphoreType.DMA((10,)),
        ],
        compiler_params=pltpu.CompilerParams(
            collective_id=0, has_side_effects=True, vmem_limit_bytes=48 << 20
        ),
        name="advect",
    )(
        tracers.reshape(2 * flat, COLS),
        east_courant.reshape(flat, COLS),
        north_courant.reshape(flat, COLS),
        diffusivity.reshape(flat, COLS),
        wet_levels,
    )
    return result.reshape(2, LEVELS, ROWS, COLS)


def solution(mesh):
    placed = (
        P(None, None, "lat", "lon"),
        P(None, "lat", "lon"),
        P(None, "lat", "lon"),
        P(None, "lat", "lon"),
        P("lat", "lon"),
    )
    return jax.shard_map(
        functools.partial(per_device, mesh.shape["lon"], mesh.shape["lat"]),
        mesh=mesh,
        in_specs=placed,
        out_specs=P(None, None, "lat", "lon"),
        check_vma=False,
    )
```

```python
import functools

import jax
import jax.numpy as jnp
from jax import lax
from jax.experimental import pallas as pl
from jax.experimental.pallas import tpu as pltpu
from jax.sharding import PartitionSpec as P

MESH = pl.DeviceIdType.MESH
LEVELS, ROWS, COLS = 8, 48, 128
PAD = 8
SPAN = ROWS + 2 * PAD
REACH = 6
T0, T1, EAST, NORTH, KAPPA, WET = range(6)
SLOTS = ((6, 6), (6, 12), (5, 17), (4, 21), (5, 26), (5, 31))


def roll(value, shift):
    return pltpu.roll(value, shift % COLS, 1)


def lane_index():
    return lax.broadcasted_iota(jnp.int32, (LEVELS, COLS), 1)


def reverse(value):
    return jnp.take_along_axis(value, COLS - 1 - lane_index(), axis=1, mode="promise_in_bounds")


def face(speed, kappa_sum, mask):
    speed = speed * mask
    magnitude = jnp.abs(speed)
    return (
        speed,
        jnp.minimum(speed, 0.0) - 0.5 * kappa_sum * mask,
        0.5 * magnitude * (1.0 - magnitude),
    )


def flux(cell, before, here, after, coef):
    speed, drift, limit = coef
    upslope = jnp.where(speed > 0, before, after)
    limited = jnp.minimum(jnp.maximum(upslope, jnp.minimum(here, 0.0)), jnp.maximum(here, 0.0))
    return speed * cell + drift * here + limit * limited


def coefficients(row, east, north, kappa, wet, out):
    here, above = kappa(row), kappa(row + 1)
    wet_here, wet_above = wet(row), wet(row + 1)
    along = face(east(row), here + roll(here, -1), wet_here * roll(wet_here, -1))
    across = face(north(row), here + above, wet_here * wet_above)
    for number, value in enumerate(along + across):
        out[row, number] = value


def advance(source, coef, start, count, store, width):
    def north_flux(row, tracer, cell, diffs):
        return flux(cell, *diffs, tuple(coef[row, 3 + k] for k in range(3)))

    def first_flux(tracer):
        cells = [source(start - 2 + k, tracer) for k in range(4)]
        diffs = [cells[k + 1] - cells[k] for k in range(3)]
        return north_flux(start - 1, tracer, cells[1], diffs)

    def body(number, below):
        base = start + number * width
        below = list(below)
        for tracer in range(2):
            cells = [source(base - 1 + k, tracer) for k in range(width + 3)]
            diffs = [cells[k + 1] - cells[k] for k in range(width + 2)]
            for k in range(width):
                row = base + k
                cell = cells[k + 1]
                here = roll(cell, -1) - cell
                along = flux(
                    cell, roll(here, 1), here, roll(here, -1), tuple(coef[row, i] for i in range(3))
                )
                across = north_flux(row, tracer, cell, diffs[k : k + 3])
                store(row, tracer, cell - (along - roll(along, 1)) - (across - below[tracer]))
                below[tracer] = across
        return tuple(below)

    below = (first_flux(0), first_flux(1))
    if count == width:
        body(0, below)
    else:
        lax.fori_loop(0, count // width, body, below)


def kernel(
    nlon, nlat,
    tracers_hbm, east_hbm, north_hbm, kappa_hbm, levels_hbm, out_ref,
    tracers_in, east_in, north_in, kappa_in, levels,
    cells, wet, to_east, to_west, from_west, from_east, strip,
    main_coef, strip_coef, main_1, main_2, main_3, strip_1, strip_2,
    load_sem, send_sem, recv_sem,
):
    lon, lat = lax.axis_index("lon"), lax.axis_index("lat")
    at_top, at_bottom = lat == nlat - 1, lat == 0
    below_top, above_bottom = jnp.logical_not(at_top), jnp.logical_not(at_bottom)
    east_lon, west_lon = lax.rem(lon + 1, nlon), lax.rem(lon + nlon - 1, nlon)
    fold_lon, fold_east, fold_west = nlon - 1 - lon, nlon - 1 - east_lon, nlon - 1 - west_lon
    east_is_self = jnp.logical_and(at_top, fold_east == lon)
    west_is_self = jnp.logical_and(at_top, fold_west == lon)
    lane = lane_index()

    north_lat = jnp.where(at_top, lat, lat + 1)
    south_lat = jnp.where(at_bottom, lat, lat - 1)
    north = (jnp.where(at_top, fold_lon, lon), north_lat)
    north_east = (jnp.where(at_top, fold_east, east_lon), north_lat)
    north_west = (jnp.where(at_top, fold_west, west_lon), north_lat)
    south, south_east, south_west = (lon, south_lat), (east_lon, south_lat), (west_lon, south_lat)

    partners = (
        ((east_lon, lat), None),
        ((west_lon, lat), None),
        (north, None),
        (north_east, jnp.logical_not(east_is_self)),
        (north_west, jnp.logical_not(west_is_self)),
        (south, above_bottom),
        (south_east, above_bottom),
        (south_west, above_bottom),
    )

    def under(condition, action):
        if condition is None:
            action()
        else:
            pl.when(condition)(action)

    barrier = pltpu.get_barrier_semaphore()
    for device, condition in partners:
        under(
            condition,
            lambda device=device: pl.semaphore_signal(
                barrier, 1, device_id=device, device_id_type=MESH
            ),
        )

    loads = [
        pltpu.make_async_copy(source, target, load_sem.at[number])
        for number, (source, target) in enumerate(
            (
                (levels_hbm, levels.at[pl.ds(PAD, ROWS)]),
                (tracers_hbm, tracers_in),
                (east_hbm, east_in),
                (north_hbm, north_in),
                (kappa_hbm, kappa_in),
            )
        )
    ]
    for copy in loads:
        copy.start()

    @pl.when(at_bottom)
    def _():
        zero = jnp.zeros((LEVELS, COLS), jnp.float32)
        levels[pl.ds(0, PAD)] = jnp.zeros((PAD, COLS), jnp.int32)
        for row in range(PAD - REACH, PAD):
            for number in range(5):
                cells[row, number] = zero
        for number in range(2):
            from_west[number] = zero
            from_east[number] = zero

    for copy in loads:
        copy.wait()

    depth = lax.broadcasted_iota(jnp.int32, (LEVELS, COLS), 0)

    def wet_row(row):
        return (depth < levels[pl.ds(row, 1)]).astype(jnp.float32)

    def gather(number):
        eastern = jnp.zeros((LEVELS, COLS), jnp.float32)
        western = jnp.zeros((LEVELS, COLS), jnp.float32)
        for group in range(4):
            row = number * 4 + group
            values = [
                tracers_in[pl.ds(row, LEVELS, stride=ROWS)],
                tracers_in[pl.ds(row + LEVELS * ROWS, LEVELS, stride=ROWS)],
                east_in[pl.ds(row, LEVELS, stride=ROWS)],
                north_in[pl.ds(row, LEVELS, stride=ROWS)],
                kappa_in[pl.ds(row, LEVELS, stride=ROWS)],
                wet_row(row + PAD),
            ]
            for which in range(5):
                cells[row + PAD, which] = values[which]
            wet[row + PAD] = values[WET]
            for which, (width, end) in enumerate(SLOTS):
                last = 32 * group + end
                inside = jnp.logical_and(lane >= last - width, lane < last)
                eastern = jnp.where(inside, roll(values[which], last), eastern)
                start = 32 * group + 32 - end
                inside = jnp.logical_and(lane >= start, lane < start + width)
                western = jnp.where(inside, roll(values[which], start), western)
        to_east[number] = eastern
        to_west[number] = western

    def gather_pair(pair, carry):
        gather(2 * pair)
        gather(2 * pair + 1)
        return carry

    lax.fori_loop(0, ROWS // 8, gather_pair, 0)

    count = 3 + sum(
        condition.astype(jnp.int32) for _, condition in partners if condition is not None
    )
    pl.semaphore_wait(barrier, count)

    own = pl.ds(2, ROWS // 4)
    low, high = pl.ds(0, 2), pl.ds(2 + ROWS // 4, 2)
    top_groups = pl.ds(ROWS // 4 - 2, 2)
    low_rows, high_rows = pl.ds(PAD - REACH, REACH), pl.ds(PAD + ROWS, REACH)
    first_rows, last_rows = pl.ds(PAD, REACH), pl.ds(PAD + ROWS - REACH, REACH)

    def remote(source, target, send, receive, device):
        return pltpu.make_async_remote_copy(
            src_ref=source,
            dst_ref=target,
            send_sem=send_sem.at[send],
            recv_sem=recv_sem.at[receive],
            device_id=device,
            device_id_type=MESH,
        )

    remote(to_east, from_west.at[own], 0, 0, (east_lon, lat)).start()
    remote(to_west, from_east.at[own], 1, 1, (west_lon, lat)).start()

    @pl.when(at_top)
    def _():
        remote(cells.at[last_rows], cells.at[high_rows], 6, 7, north).start()
        remote(levels.at[pl.ds(ROWS, 8)], levels.at[pl.ds(PAD + ROWS, 8)], 8, 9, north).start()

        @pl.when(jnp.logical_not(east_is_self))
        def _():
            remote(to_east.at[top_groups], from_east.at[high], 2, 5, north_east).start()

        @pl.when(jnp.logical_not(west_is_self))
        def _():
            remote(to_west.at[top_groups], from_west.at[high], 3, 4, north_west).start()

        @pl.when(east_is_self)
        def _():
            from_east[high] = to_east[top_groups]

        @pl.when(west_is_self)
        def _():
            from_west[high] = to_west[top_groups]

    @pl.when(below_top)
    def _():
        remote(to_east.at[top_groups], from_west.at[low], 2, 2, north_east).start()
        remote(to_west.at[top_groups], from_east.at[low], 3, 3, north_west).start()

    @pl.when(above_bottom)
    def _():
        remote(to_east.at[low], from_west.at[high], 4, 4, south_east).start()
        remote(to_west.at[low], from_east.at[high], 5, 5, south_west).start()
        remote(levels.at[pl.ds(PAD, 8)], levels.at[pl.ds(PAD + ROWS, 8)], 9, 9, south).start()
        remote(cells.at[first_rows], cells.at[high_rows], 7, 7, south).start()

    @pl.when(below_top)
    def _():
        remote(levels.at[pl.ds(ROWS, 8)], levels.at[pl.ds(0, 8)], 8, 8, north).start()
        remote(cells.at[last_rows], cells.at[low_rows], 6, 6, north).start()


    def folded(value):
        return jnp.where(lane < COLS // 2, roll(value, REACH), roll(value, -REACH))

    def strip_own(number, carry):
        for k in range(8):
            row = PAD + 8 * number + k
            for which in range(5):
                strip[row, which] = folded(cells[row, which])
            strip[row, WET] = folded(wet[row])
        return carry

    lax.fori_loop(0, ROWS // 8, strip_own, 0)

    main_parts = (
        lambda row: cells[row, EAST],
        lambda row: cells[row, NORTH],
        lambda row: cells[row, KAPPA],
        lambda row: wet[row],
    )
    strip_parts = tuple(
        lambda row, which=which: strip[row, which] for which in (EAST, NORTH, KAPPA, WET)
    )

    def main_coefficients(number, carry):
        for k in range(9):
            coefficients(PAD + 1 + 9 * number + k, *main_parts, main_coef)
        return carry

    lax.fori_loop(0, 5, main_coefficients, 0)

    def keep(target):
        def store(row, tracer, value):
            target[row, tracer] = value

        return store

    def reading(source):
        return lambda row, tracer: source[row, tracer]

    stages = (reading(cells), reading(main_1), reading(main_2))
    targets = (keep(main_1), keep(main_2), keep(main_3))
    for step, width in enumerate((11, 10, 12)):
        margin = 2 * (step + 1)
        advance(stages[step], main_coef, PAD + margin, ROWS - 2 * margin, targets[step], width)


    def arrival(slot, target):
        remote(target, target, slot, slot, (lon, lat)).wait_recv()

    def departure(slot, source):
        remote(source, source, slot, slot, (lon, lat)).wait_send()

    arrival(7, cells.at[high_rows])
    arrival(9, levels.at[pl.ds(PAD + ROWS, 8)])
    departure(6, cells.at[last_rows])
    departure(8, levels.at[pl.ds(ROWS, 8)])

    @pl.when(above_bottom)
    def _():
        arrival(6, cells.at[low_rows])
        arrival(8, levels.at[pl.ds(0, 8)])
        departure(7, cells.at[first_rows])
        departure(9, levels.at[pl.ds(PAD, 8)])

    north_start = PAD + ROWS
    raw_start = jnp.where(at_top, north_start + 2, north_start)
    for k in range(REACH):
        wet[PAD - REACH + k] = wet_row(PAD - REACH + k)
        wet[north_start + k] = wet_row(raw_start + k)

    @pl.when(at_top)
    def _():
        def swap(k, carry):
            one, other = north_start + k, north_start + REACH - 1 - k
            for which in range(5):
                near, far = cells[one, which], cells[other, which]
                cells[one, which], cells[other, which] = reverse(far), reverse(near)
            near, far = wet[one], wet[other]
            wet[one], wet[other] = reverse(far), reverse(near)
            return carry

        lax.fori_loop(0, REACH // 2, swap, 0)

    def strip_ghost(k, carry):
        for row in (PAD - REACH + k, north_start + k):
            for which in range(5):
                strip[row, which] = folded(cells[row, which])
            strip[row, WET] = folded(wet[row])
        return carry

    lax.fori_loop(0, REACH, strip_ghost, 0)

    def fold_speeds(part):
        last = north_start - 1
        part[last, NORTH] = 0.5 * (part[last, NORTH] - part[north_start, NORTH])
        for k in range(4):
            row = north_start + k
            part[row, NORTH] = -part[row + 1, NORTH]
            part[row, EAST] = -roll(part[row, EAST], -1)

    pl.when(at_top)(lambda: fold_speeds(cells))

    for row in (3, 4, 5, 6, 7, 8, 54, 55, 56, 57, 58, 59):
        coefficients(row, *main_parts, main_coef)

    for step in range(3):
        reach = REACH - 2 * (step + 1)
        advance(stages[step], main_coef, PAD - reach, REACH, targets[step], REACH)
        advance(stages[step], main_coef, PAD + ROWS - 2 * (step + 1), REACH, targets[step], REACH)

    @pl.when(above_bottom)
    def _():
        arrival(2, from_west.at[low])
        arrival(3, from_east.at[low])
        departure(4, to_east.at[low])
        departure(5, to_west.at[low])

    @pl.when(jnp.logical_not(west_is_self))
    def _():
        arrival(4, from_west.at[high])
        departure(3, to_west.at[top_groups])

    @pl.when(jnp.logical_not(east_is_self))
    def _():
        arrival(5, from_east.at[high])
        departure(2, to_east.at[top_groups])

    @pl.when(at_top)
    def _():
        for side in (from_west, from_east):
            lower, upper = side[2 + ROWS // 4], side[3 + ROWS // 4]
            side[2 + ROWS // 4], side[3 + ROWS // 4] = reverse(upper), reverse(lower)

    arrival(0, from_west.at[own])
    arrival(1, from_east.at[own])
    departure(0, to_east)
    departure(1, to_west)

    def edged(row_group, groups):
        for group in groups:
            row = 4 * row_group + group
            for which, (_, end) in enumerate(SLOTS):
                left = roll(from_west[row_group], REACH - 32 * group - end)
                right = roll(from_east[row_group], COLS - REACH - 32 - 32 * group + end)
                strip[row, which] = jnp.where(
                    lane < REACH, left, jnp.where(lane >= COLS - REACH, right, strip[row, which])
                )

    def strip_edges(number, carry):
        edged(1 + 2 * number, range(4))
        edged(2 + 2 * number, range(4))
        return carry

    edged(0, (2, 3))
    lax.fori_loop(0, 7, strip_edges, 0)
    edged(SPAN // 4 - 1, (0, 1))

    pl.when(at_top)(lambda: fold_speeds(strip))

    def strip_coefficients(number, carry):
        for k in range(19):
            coefficients(3 + 19 * number + k, *strip_parts, strip_coef)
        return carry

    lax.fori_loop(0, 3, strip_coefficients, 0)

    advance(reading(strip), strip_coef, PAD - 4, ROWS + 8, keep(strip_1), 14)
    advance(reading(strip_1), strip_coef, PAD - 2, ROWS + 4, keep(strip_2), 13)

    def finish(row, tracer, value):
        merged = jnp.where(
            lane < REACH,
            roll(value, -REACH),
            jnp.where(lane >= COLS - REACH, roll(value, REACH), main_3[row, tracer]),
        )
        out_ref[pl.ds(tracer * LEVELS * ROWS + row - PAD, LEVELS, stride=ROWS)] = merged

    advance(reading(strip_2), strip_coef, PAD, ROWS, finish, 12)


def per_device(nlon, nlat, tracers, east_courant, north_courant, diffusivity, wet_levels):
    flat = LEVELS * ROWS
    f32 = jnp.float32
    vreg = (LEVELS, COLS)
    result = pl.pallas_call(
        functools.partial(kernel, nlon, nlat),
        out_shape=pltpu.VMEM((2 * flat, COLS), f32),
        in_specs=[pl.BlockSpec(memory_space=pl.ANY)] * 5,
        out_specs=pl.BlockSpec(memory_space=pltpu.VMEM),
        scratch_shapes=[
            pltpu.VMEM((2 * flat, COLS), f32),
            pltpu.VMEM((flat, COLS), f32),
            pltpu.VMEM((flat, COLS), f32),
            pltpu.VMEM((flat, COLS), f32),
            pltpu.VMEM((SPAN, COLS), jnp.int32),
            pltpu.VMEM((SPAN, 5) + vreg, f32),
            pltpu.VMEM((SPAN,) + vreg, f32),
            pltpu.VMEM((ROWS // 4,) + vreg, f32),
            pltpu.VMEM((ROWS // 4,) + vreg, f32),
            pltpu.VMEM((SPAN // 4,) + vreg, f32),
            pltpu.VMEM((SPAN // 4,) + vreg, f32),
            pltpu.VMEM((SPAN, 6) + vreg, f32),
            pltpu.VMEM((SPAN, 6) + vreg, f32),
            pltpu.VMEM((SPAN, 6) + vreg, f32),
            pltpu.VMEM((SPAN, 2) + vreg, f32),
            pltpu.VMEM((SPAN, 2) + vreg, f32),
            pltpu.VMEM((SPAN, 2) + vreg, f32),
            pltpu.VMEM((SPAN, 2) + vreg, f32),
            pltpu.VMEM((SPAN, 2) + vreg, f32),
            pltpu.SemaphoreType.DMA((5,)),
            pltpu.SemaphoreType.DMA((10,)),
            pltpu.SemaphoreType.DMA((10,)),
        ],
        compiler_params=pltpu.CompilerParams(
            collective_id=0, has_side_effects=True, vmem_limit_bytes=56 << 20
        ),
        name="advect",
    )(
        tracers.reshape(2 * flat, COLS),
        east_courant.reshape(flat, COLS),
        north_courant.reshape(flat, COLS),
        diffusivity.reshape(flat, COLS),
        wet_levels,
    )
    return result.reshape(2, LEVELS, ROWS, COLS)


def solution(mesh):
    placed = (
        P(None, None, "lat", "lon"),
        P(None, "lat", "lon"),
        P(None, "lat", "lon"),
        P(None, "lat", "lon"),
        P("lat", "lon"),
    )
    return jax.shard_map(
        functools.partial(per_device, mesh.shape["lon"], mesh.shape["lat"]),
        mesh=mesh,
        in_specs=placed,
        out_specs=P(None, None, "lat", "lon"),
        check_vma=False,
    )
```

```python
import functools

import jax
import jax.numpy as jnp
from jax import lax
from jax.experimental import pallas as pl
from jax.experimental.pallas import tpu as pltpu
from jax.sharding import PartitionSpec as P

MESH = pl.DeviceIdType.MESH
LEVELS, ROWS, COLS = 8, 48, 128
PAD = 8
SPAN = ROWS + 2 * PAD
REACH = 6
GROUPS, LANES = 4, 32
STRIDE = ROWS // GROUPS
STRIPS = STRIDE + 2 * REACH
T0, T1, EAST, NORTH, KAPPA, WET = range(6)
SLOTS = ((6, 6), (6, 12), (5, 17), (4, 21), (5, 26), (5, 31))


def roll(value, shift):
    return pltpu.roll(value, shift % COLS, 1)


def lane_index():
    return lax.broadcasted_iota(jnp.int32, (LEVELS, COLS), 1)


def reverse(value):
    return jnp.take_along_axis(value, COLS - 1 - lane_index(), axis=1, mode="promise_in_bounds")


def face(speed, kappa_sum, mask):
    speed = speed * mask
    magnitude = jnp.abs(speed)
    return (
        speed,
        jnp.minimum(speed, 0.0) - 0.5 * kappa_sum * mask,
        0.5 * magnitude * (1.0 - magnitude),
    )


def flux(cell, before, here, after, coef):
    speed, drift, limit = coef
    upslope = jnp.where(speed > 0, before, after)
    limited = jnp.minimum(jnp.maximum(upslope, jnp.minimum(here, 0.0)), jnp.maximum(here, 0.0))
    return speed * cell + drift * here + limit * limited


def coefficients(row, east, north, kappa, wet, out):
    here, above = kappa(row), kappa(row + 1)
    wet_here, wet_above = wet(row), wet(row + 1)
    along = face(east(row), here + roll(here, -1), wet_here * roll(wet_here, -1))
    across = face(north(row), here + above, wet_here * wet_above)
    for number, value in enumerate(along + across):
        out[row, number] = value


def advance(source, coef, start, count, store, width):
    def north_flux(row, tracer, cell, diffs):
        return flux(cell, *diffs, tuple(coef[row, 3 + k] for k in range(3)))

    def first_flux(tracer):
        cells = [source(start - 2 + k, tracer) for k in range(4)]
        diffs = [cells[k + 1] - cells[k] for k in range(3)]
        return north_flux(start - 1, tracer, cells[1], diffs)

    def body(number, below):
        base = start + number * width
        below = list(below)
        for tracer in range(2):
            cells = [source(base - 1 + k, tracer) for k in range(width + 3)]
            diffs = [cells[k + 1] - cells[k] for k in range(width + 2)]
            for k in range(width):
                row = base + k
                cell = cells[k + 1]
                here = roll(cell, -1) - cell
                along = flux(
                    cell, roll(here, 1), here, roll(here, -1), tuple(coef[row, i] for i in range(3))
                )
                across = north_flux(row, tracer, cell, diffs[k : k + 3])
                store(row, tracer, cell - (along - roll(along, 1)) - (across - below[tracer]))
                below[tracer] = across
        return tuple(below)

    below = (first_flux(0), first_flux(1))
    if count == width:
        body(0, below)
    else:
        lax.fori_loop(0, count // width, body, below)


def kernel(
    nlon, nlat,
    tracers_hbm, east_hbm, north_hbm, kappa_hbm, levels_hbm, out_ref,
    tracers_in, east_in, north_in, kappa_in, levels,
    cells, wet, to_east, to_west, corner_east, corner_west, from_west, from_east, strip,
    main_coef, strip_coef, main_1, main_2, main_3, strip_in, strip_1, strip_2,
    load_sem, send_sem, recv_sem,
):
    lon, lat = lax.axis_index("lon"), lax.axis_index("lat")
    at_top, at_bottom = lat == nlat - 1, lat == 0
    below_top, above_bottom = jnp.logical_not(at_top), jnp.logical_not(at_bottom)
    east_lon, west_lon = lax.rem(lon + 1, nlon), lax.rem(lon + nlon - 1, nlon)
    fold_lon, fold_east, fold_west = nlon - 1 - lon, nlon - 1 - east_lon, nlon - 1 - west_lon
    east_is_self = jnp.logical_and(at_top, fold_east == lon)
    west_is_self = jnp.logical_and(at_top, fold_west == lon)
    lane = lane_index()

    north_lat = jnp.where(at_top, lat, lat + 1)
    south_lat = jnp.where(at_bottom, lat, lat - 1)
    north = (jnp.where(at_top, fold_lon, lon), north_lat)
    north_east = (jnp.where(at_top, fold_east, east_lon), north_lat)
    north_west = (jnp.where(at_top, fold_west, west_lon), north_lat)
    south, south_east, south_west = (lon, south_lat), (east_lon, south_lat), (west_lon, south_lat)

    partners = (
        ((east_lon, lat), None),
        ((west_lon, lat), None),
        (north, None),
        (north_east, jnp.logical_not(east_is_self)),
        (north_west, jnp.logical_not(west_is_self)),
        (south, above_bottom),
        (south_east, above_bottom),
        (south_west, above_bottom),
    )

    def under(condition, action):
        if condition is None:
            action()
        else:
            pl.when(condition)(action)

    barrier = pltpu.get_barrier_semaphore()
    for device, condition in partners:
        under(
            condition,
            lambda device=device: pl.semaphore_signal(
                barrier, 1, device_id=device, device_id_type=MESH
            ),
        )

    loads = [
        pltpu.make_async_copy(source, target, load_sem.at[number])
        for number, (source, target) in enumerate(
            (
                (levels_hbm, levels.at[pl.ds(PAD, ROWS)]),
                (tracers_hbm, tracers_in),
                (east_hbm, east_in),
                (north_hbm, north_in),
                (kappa_hbm, kappa_in),
            )
        )
    ]
    for copy in loads:
        copy.start()

    @pl.when(at_bottom)
    def _():
        zero = jnp.zeros((LEVELS, COLS), jnp.float32)
        levels[pl.ds(0, PAD)] = jnp.zeros((PAD, COLS), jnp.int32)
        for row in range(PAD - REACH, PAD):
            for number in range(5):
                cells[row, number] = zero
        for number in range(2):
            from_west[number] = zero
            from_east[number] = zero

    for copy in loads:
        copy.wait()

    depth = lax.broadcasted_iota(jnp.int32, (LEVELS, COLS), 0)

    def wet_row(row):
        return (depth < levels[pl.ds(row, 1)]).astype(jnp.float32)

    def gather(number):
        eastern = jnp.zeros((LEVELS, COLS), jnp.float32)
        western = jnp.zeros((LEVELS, COLS), jnp.float32)
        for group in range(GROUPS):
            row = number + STRIDE * group
            values = [
                tracers_in[pl.ds(row, LEVELS, stride=ROWS)],
                tracers_in[pl.ds(row + LEVELS * ROWS, LEVELS, stride=ROWS)],
                east_in[pl.ds(row, LEVELS, stride=ROWS)],
                north_in[pl.ds(row, LEVELS, stride=ROWS)],
                kappa_in[pl.ds(row, LEVELS, stride=ROWS)],
                wet_row(row + PAD),
            ]
            for which in range(5):
                cells[row + PAD, which] = values[which]
            wet[row + PAD] = values[WET]
            for which, (width, end) in enumerate(SLOTS):
                last = LANES * group + end
                inside = jnp.logical_and(lane >= last - width, lane < last)
                eastern = jnp.where(inside, roll(values[which], last), eastern)
                start = LANES * (group + 1) - end
                inside = jnp.logical_and(lane >= start, lane < start + width)
                western = jnp.where(inside, roll(values[which], start), western)
        to_east[number] = eastern
        to_west[number] = western

    def gather_pair(pair, carry):
        gather(2 * pair)
        gather(2 * pair + 1)
        return carry

    lax.fori_loop(0, STRIDE // 2, gather_pair, 0)

    for side, corner in ((to_east, corner_east), (to_west, corner_west)):
        for number, rows in enumerate((range(0, 4), range(4, 6), range(ROWS - 6, ROWS - 4), range(ROWS - 4, ROWS))):
            packed = side[rows[0] % STRIDE]
            for row in rows:
                moved = roll(side[row % STRIDE], LANES * (row % GROUPS - row // STRIDE))
                packed = jnp.where(lane // LANES == row % GROUPS, moved, packed)
            corner[number] = packed

    count = 3 + sum(
        condition.astype(jnp.int32) for _, condition in partners if condition is not None
    )
    pl.semaphore_wait(barrier, count)

    own = pl.ds(2, STRIDE)
    low, high = pl.ds(0, 2), pl.ds(2 + STRIDE, 2)
    high_corner = pl.ds(2, 2)
    low_rows, high_rows = pl.ds(PAD - REACH, REACH), pl.ds(PAD + ROWS, REACH)
    first_rows, last_rows = pl.ds(PAD, REACH), pl.ds(PAD + ROWS - REACH, REACH)

    def remote(source, target, send, receive, device):
        return pltpu.make_async_remote_copy(
            src_ref=source,
            dst_ref=target,
            send_sem=send_sem.at[send],
            recv_sem=recv_sem.at[receive],
            device_id=device,
            device_id_type=MESH,
        )

    remote(to_east, from_west.at[own], 0, 0, (east_lon, lat)).start()
    remote(to_west, from_east.at[own], 1, 1, (west_lon, lat)).start()

    @pl.when(at_top)
    def _():
        remote(cells.at[last_rows], cells.at[high_rows], 6, 7, north).start()
        remote(levels.at[pl.ds(ROWS, 8)], levels.at[pl.ds(PAD + ROWS, 8)], 8, 9, north).start()

        @pl.when(jnp.logical_not(east_is_self))
        def _():
            remote(corner_east.at[high_corner], from_east.at[high], 2, 5, north_east).start()

        @pl.when(jnp.logical_not(west_is_self))
        def _():
            remote(corner_west.at[high_corner], from_west.at[high], 3, 4, north_west).start()

        @pl.when(east_is_self)
        def _():
            from_east[high] = corner_east[high_corner]

        @pl.when(west_is_self)
        def _():
            from_west[high] = corner_west[high_corner]

    @pl.when(below_top)
    def _():
        remote(corner_east.at[high_corner], from_west.at[low], 2, 2, north_east).start()
        remote(corner_west.at[high_corner], from_east.at[low], 3, 3, north_west).start()

    @pl.when(above_bottom)
    def _():
        remote(corner_east.at[low], from_west.at[high], 4, 4, south_east).start()
        remote(corner_west.at[low], from_east.at[high], 5, 5, south_west).start()
        remote(levels.at[pl.ds(PAD, 8)], levels.at[pl.ds(PAD + ROWS, 8)], 9, 9, south).start()
        remote(cells.at[first_rows], cells.at[high_rows], 7, 7, south).start()

    @pl.when(below_top)
    def _():
        remote(levels.at[pl.ds(ROWS, 8)], levels.at[pl.ds(0, 8)], 8, 8, north).start()
        remote(cells.at[last_rows], cells.at[low_rows], 6, 6, north).start()


    group_lane = lane % LANES
    left_halo, right_halo = group_lane < REACH, group_lane >= LANES - REACH
    to_left, to_right = REACH, LANES - REACH

    def edges(value, group):
        return jnp.where(
            lane < LANES * group + LANES // 2,
            roll(value, LANES * group + to_left),
            roll(value, LANES * group + to_right),
        )

    def packed_rows(read):
        total = edges(read(0), 0)
        for group in range(1, GROUPS):
            total = jnp.where(lane // LANES == group, edges(read(group), group), total)
        return total

    def strip_own(number, carry):
        for k in range(2):
            first = PAD + 2 * number + k
            target = REACH + 2 * number + k
            for which in range(5):
                strip[target, which] = packed_rows(
                    lambda group, which=which: cells[first + STRIDE * group, which]
                )
            strip[target, WET] = packed_rows(lambda group: wet[first + STRIDE * group])
        return carry

    lax.fori_loop(0, STRIDE // 2, strip_own, 0)

    main_parts = (
        lambda row: cells[row, EAST],
        lambda row: cells[row, NORTH],
        lambda row: cells[row, KAPPA],
        lambda row: wet[row],
    )
    strip_parts = tuple(
        lambda row, which=which: strip[row, which] for which in (EAST, NORTH, KAPPA, WET)
    )

    def main_coefficients(number, carry):
        for k in range(9):
            coefficients(PAD + 1 + 9 * number + k, *main_parts, main_coef)
        return carry

    lax.fori_loop(0, 5, main_coefficients, 0)

    def keep(target):
        def store(row, tracer, value):
            target[row, tracer] = value

        return store

    def reading(source):
        return lambda row, tracer: source[row, tracer]

    stages = (reading(cells), reading(main_1), reading(main_2))
    targets = (keep(main_1), keep(main_2), keep(main_3))
    for step, width in enumerate((11, 10, 12)):
        margin = 2 * (step + 1)
        advance(stages[step], main_coef, PAD + margin, ROWS - 2 * margin, targets[step], width)


    def arrival(slot, target):
        remote(target, target, slot, slot, (lon, lat)).wait_recv()

    def departure(slot, source):
        remote(source, source, slot, slot, (lon, lat)).wait_send()

    arrival(7, cells.at[high_rows])
    arrival(9, levels.at[pl.ds(PAD + ROWS, 8)])
    departure(6, cells.at[last_rows])
    departure(8, levels.at[pl.ds(ROWS, 8)])

    @pl.when(above_bottom)
    def _():
        arrival(6, cells.at[low_rows])
        arrival(8, levels.at[pl.ds(0, 8)])
        departure(7, cells.at[first_rows])
        departure(9, levels.at[pl.ds(PAD, 8)])

    north_start = PAD + ROWS
    raw_start = jnp.where(at_top, north_start + 2, north_start)
    for k in range(REACH):
        wet[PAD - REACH + k] = wet_row(PAD - REACH + k)
        wet[north_start + k] = wet_row(raw_start + k)

    @pl.when(at_top)
    def _():
        def swap(k, carry):
            one, other = north_start + k, north_start + REACH - 1 - k
            for which in range(5):
                near, far = cells[one, which], cells[other, which]
                cells[one, which], cells[other, which] = reverse(far), reverse(near)
            near, far = wet[one], wet[other]
            wet[one], wet[other] = reverse(far), reverse(near)
            return carry

        lax.fori_loop(0, REACH // 2, swap, 0)

    def strip_ghost(k, carry):
        for which in range(6):
            def read(row, which=which):
                return wet[row] if which == WET else cells[row, which]

            below = roll(strip[STRIDE + k, which], LANES)
            strip[k, which] = jnp.where(lane < LANES, edges(read(PAD - REACH + k), 0), below)
            above = roll(strip[REACH + k, which], -LANES)
            strip[REACH + STRIDE + k, which] = jnp.where(
                lane >= COLS - LANES, edges(read(north_start + k), GROUPS - 1), above
            )
        return carry

    lax.fori_loop(0, REACH, strip_ghost, 0)

    def fold_speeds(part, last, where):
        part[last, NORTH] = where(0.5 * (part[last, NORTH] - part[last + 1, NORTH]), part[last, NORTH])
        for k in range(1, 5):
            row = last + k
            part[row, NORTH] = where(-part[row + 1, NORTH], part[row, NORTH])
            part[row, EAST] = where(-roll(part[row, EAST], -1), part[row, EAST])

    pl.when(at_top)(lambda: fold_speeds(cells, north_start - 1, lambda new, old: new))

    for row in (3, 4, 5, 6, 7, 8, 54, 55, 56, 57, 58, 59):
        coefficients(row, *main_parts, main_coef)

    for step in range(3):
        reach = REACH - 2 * (step + 1)
        advance(stages[step], main_coef, PAD - reach, REACH, targets[step], REACH)
        advance(stages[step], main_coef, PAD + ROWS - 2 * (step + 1), REACH, targets[step], REACH)

    def inner(k, carry):
        for tracer in range(2):
            near = packed_rows(lambda group: main_1[PAD + k + STRIDE * group, tracer])
            strip_in[REACH + k, tracer] = near
        return carry

    lax.fori_loop(0, STRIDE, inner, 0)
    for k in range(4):
        for tracer in range(2):
            strip_in[2 + k, tracer] = jnp.where(
                lane < LANES,
                edges(main_1[PAD - 4 + k, tracer], 0),
                roll(strip_in[STRIDE + 2 + k, tracer], LANES),
            )
            strip_in[REACH + STRIDE + k, tracer] = jnp.where(
                lane >= COLS - LANES,
                edges(main_1[north_start + k, tracer], GROUPS - 1),
                roll(strip_in[REACH + k, tracer], -LANES),
            )

    @pl.when(above_bottom)
    def _():
        arrival(2, from_west.at[low])
        arrival(3, from_east.at[low])
        departure(4, corner_east.at[low])
        departure(5, corner_west.at[low])

    @pl.when(jnp.logical_not(west_is_self))
    def _():
        arrival(4, from_west.at[high])
        departure(3, corner_west.at[high_corner])

    @pl.when(jnp.logical_not(east_is_self))
    def _():
        arrival(5, from_east.at[high])
        departure(2, corner_east.at[high_corner])

    @pl.when(at_top)
    def _():
        for side in (from_west, from_east):
            lower, upper = side[2 + STRIDE], side[3 + STRIDE]
            side[2 + STRIDE], side[3 + STRIDE] = reverse(upper), reverse(lower)

    arrival(0, from_west.at[own])
    arrival(1, from_east.at[own])
    departure(0, to_east)
    departure(1, to_west)

    def halo(number, shift, which):
        end = SLOTS[which][1]
        return jnp.where(
            left_halo,
            roll(from_west[number], shift + REACH - end),
            roll(from_east[number], shift + end - REACH),
        )

    outside = jnp.logical_or(left_halo, right_halo)

    def strip_edges(number, carry):
        for k in range(6):
            place = 6 * number + k
            for which in range(6):
                strip[REACH + place, which] = jnp.where(
                    outside, halo(2 + place, 0, which), strip[REACH + place, which]
                )
        return carry

    lax.fori_loop(0, STRIDE // 6, strip_edges, 0)

    for k in range(REACH):
        for which in range(6):
            corner = halo((2 + k) // 4, -LANES * ((2 + k) % 4), which)
            below = halo(2 + STRIDE - REACH + k, LANES, which)
            strip[k, which] = jnp.where(
                outside, jnp.where(lane < LANES, corner, below), strip[k, which]
            )
            corner = halo(2 + STRIDE + k // 4, LANES * (GROUPS - 1 - k % 4), which)
            above = halo(2 + k, -LANES, which)
            place = REACH + STRIDE + k
            strip[place, which] = jnp.where(
                outside, jnp.where(lane >= COLS - LANES, corner, above), strip[place, which]
            )

    @pl.when(at_top)
    def _():
        fold_speeds(
            strip, REACH + STRIDE - 1, lambda new, old: jnp.where(lane >= COLS - LANES, new, old)
        )

    for place in range(1, STRIPS - 2):
        coefficients(place, *strip_parts, strip_coef)

    lost = jnp.logical_and(group_lane >= LANES // 2 - 2, group_lane < LANES // 2 + 2)

    def first_store(place, tracer, value):
        strip_1[place, tracer] = jnp.where(lost, strip_in[place, tracer], value)

    def finish(place, tracer, value):
        for group in range(GROUPS):
            row = place - REACH + STRIDE * group
            merged = jnp.where(
                lane < REACH,
                roll(value, -LANES * group - to_left),
                jnp.where(
                    lane >= COLS - REACH,
                    roll(value, -LANES * group - to_right),
                    main_3[row + PAD, tracer],
                ),
            )
            out_ref[pl.ds(tracer * LEVELS * ROWS + row, LEVELS, stride=ROWS)] = merged

    advance(reading(strip), strip_coef, 2, STRIPS - 4, first_store, 10)
    advance(reading(strip_1), strip_coef, 4, STRIPS - 8, keep(strip_2), 8)
    advance(reading(strip_2), strip_coef, REACH, STRIDE, finish, 6)


def per_device(nlon, nlat, tracers, east_courant, north_courant, diffusivity, wet_levels):
    flat = LEVELS * ROWS
    f32 = jnp.float32
    vreg = (LEVELS, COLS)
    result = pl.pallas_call(
        functools.partial(kernel, nlon, nlat),
        out_shape=pltpu.VMEM((2 * flat, COLS), f32),
        in_specs=[pl.BlockSpec(memory_space=pl.ANY)] * 5,
        out_specs=pl.BlockSpec(memory_space=pltpu.VMEM),
        scratch_shapes=[
            pltpu.VMEM((2 * flat, COLS), f32),
            pltpu.VMEM((flat, COLS), f32),
            pltpu.VMEM((flat, COLS), f32),
            pltpu.VMEM((flat, COLS), f32),
            pltpu.VMEM((SPAN, COLS), jnp.int32),
            pltpu.VMEM((SPAN, 5) + vreg, f32),
            pltpu.VMEM((SPAN,) + vreg, f32),
            pltpu.VMEM((STRIDE,) + vreg, f32),
            pltpu.VMEM((STRIDE,) + vreg, f32),
            pltpu.VMEM((4,) + vreg, f32),
            pltpu.VMEM((4,) + vreg, f32),
            pltpu.VMEM((STRIDE + 4,) + vreg, f32),
            pltpu.VMEM((STRIDE + 4,) + vreg, f32),
            pltpu.VMEM((STRIPS, 6) + vreg, f32),
            pltpu.VMEM((SPAN, 6) + vreg, f32),
            pltpu.VMEM((STRIPS, 6) + vreg, f32),
            pltpu.VMEM((SPAN, 2) + vreg, f32),
            pltpu.VMEM((SPAN, 2) + vreg, f32),
            pltpu.VMEM((SPAN, 2) + vreg, f32),
            pltpu.VMEM((STRIPS, 2) + vreg, f32),
            pltpu.VMEM((STRIPS, 2) + vreg, f32),
            pltpu.VMEM((STRIPS, 2) + vreg, f32),
            pltpu.SemaphoreType.DMA((5,)),
            pltpu.SemaphoreType.DMA((10,)),
            pltpu.SemaphoreType.DMA((10,)),
        ],
        compiler_params=pltpu.CompilerParams(
            collective_id=0, has_side_effects=True, vmem_limit_bytes=56 << 20
        ),
        name="advect",
    )(
        tracers.reshape(2 * flat, COLS),
        east_courant.reshape(flat, COLS),
        north_courant.reshape(flat, COLS),
        diffusivity.reshape(flat, COLS),
        wet_levels,
    )
    return result.reshape(2, LEVELS, ROWS, COLS)


def solution(mesh):
    placed = (
        P(None, None, "lat", "lon"),
        P(None, "lat", "lon"),
        P(None, "lat", "lon"),
        P(None, "lat", "lon"),
        P("lat", "lon"),
    )
    return jax.shard_map(
        functools.partial(per_device, mesh.shape["lon"], mesh.shape["lat"]),
        mesh=mesh,
        in_specs=placed,
        out_specs=P(None, None, "lat", "lon"),
        check_vma=False,
    )
```

```python
import functools

import jax
import jax.numpy as jnp
from jax import lax
from jax.experimental import pallas as pl
from jax.experimental.pallas import tpu as pltpu
from jax.sharding import PartitionSpec as P

MESH = pl.DeviceIdType.MESH
LEVELS, ROWS, COLS = 8, 48, 128
PAD = 8
SPAN = ROWS + 2 * PAD
REACH = 6
GROUPS, LANES = 4, 32
STRIDE = ROWS // GROUPS
STRIPS = STRIDE + 2 * REACH
T0, T1, EAST, NORTH, KAPPA, WET = range(6)
SLOTS = ((6, 6), (6, 12), (5, 17), (4, 21), (5, 26), (5, 31))


def roll(value, shift):
    return pltpu.roll(value, shift % COLS, 1)


def lane_index():
    return lax.broadcasted_iota(jnp.int32, (LEVELS, COLS), 1)


def reverse(value):
    return jnp.take_along_axis(value, COLS - 1 - lane_index(), axis=1, mode="promise_in_bounds")


def face(speed, kappa_sum, mask):
    speed = speed * mask
    magnitude = jnp.abs(speed)
    return (
        speed,
        jnp.minimum(speed, 0.0) - 0.5 * kappa_sum * mask,
        0.5 * magnitude * (1.0 - magnitude),
    )


def flux(cell, before, here, after, coef):
    speed, drift, limit = coef
    upslope = jnp.where(speed > 0, before, after)
    limited = jnp.minimum(jnp.maximum(upslope, jnp.minimum(here, 0.0)), jnp.maximum(here, 0.0))
    return speed * cell + drift * here + limit * limited


def coefficients(row, east, north, kappa, wet, out):
    here, above = kappa(row), kappa(row + 1)
    wet_here, wet_above = wet(row), wet(row + 1)
    along = face(east(row), here + roll(here, -1), wet_here * roll(wet_here, -1))
    across = face(north(row), here + above, wet_here * wet_above)
    for number, value in enumerate(along + across):
        out[row, number] = value


def advance(source, coef, start, count, store, width):
    def north_flux(row, tracer, cell, diffs):
        return flux(cell, *diffs, tuple(coef[row, 3 + k] for k in range(3)))

    def first_flux(tracer):
        cells = [source(start - 2 + k, tracer) for k in range(4)]
        diffs = [cells[k + 1] - cells[k] for k in range(3)]
        return north_flux(start - 1, tracer, cells[1], diffs)

    def body(number, below):
        base = start + number * width
        below = list(below)
        for tracer in range(2):
            cells = [source(base - 1 + k, tracer) for k in range(width + 3)]
            diffs = [cells[k + 1] - cells[k] for k in range(width + 2)]
            for k in range(width):
                row = base + k
                cell = cells[k + 1]
                here = roll(cell, -1) - cell
                along = flux(
                    cell, roll(here, 1), here, roll(here, -1), tuple(coef[row, i] for i in range(3))
                )
                across = north_flux(row, tracer, cell, diffs[k : k + 3])
                store(row, tracer, cell - (along - roll(along, 1)) - (across - below[tracer]))
                below[tracer] = across
        return tuple(below)

    below = (first_flux(0), first_flux(1))
    if count == width:
        body(0, below)
    else:
        lax.fori_loop(0, count // width, body, below)


def kernel(
    nlon, nlat,
    tracers_hbm, east_hbm, north_hbm, kappa_hbm, levels_hbm, out_ref,
    tracers_in, east_in, north_in, kappa_in, levels,
    cells, wet, to_east, to_west, corner_east, corner_west, from_west, from_east, strip,
    main_coef, strip_coef, main_1, main_2, main_3, strip_in, strip_1, strip_2, top_speed,
    load_sem, send_sem, recv_sem,
):
    lon, lat = lax.axis_index("lon"), lax.axis_index("lat")
    at_top, at_bottom = lat == nlat - 1, lat == 0
    below_top, above_bottom = jnp.logical_not(at_top), jnp.logical_not(at_bottom)
    east_lon, west_lon = lax.rem(lon + 1, nlon), lax.rem(lon + nlon - 1, nlon)
    fold_lon, fold_east, fold_west = nlon - 1 - lon, nlon - 1 - east_lon, nlon - 1 - west_lon
    east_is_self = jnp.logical_and(at_top, fold_east == lon)
    west_is_self = jnp.logical_and(at_top, fold_west == lon)
    lane = lane_index()

    north_lat = jnp.where(at_top, lat, lat + 1)
    south_lat = jnp.where(at_bottom, lat, lat - 1)
    north = (jnp.where(at_top, fold_lon, lon), north_lat)
    north_east = (jnp.where(at_top, fold_east, east_lon), north_lat)
    north_west = (jnp.where(at_top, fold_west, west_lon), north_lat)
    south, south_east, south_west = (lon, south_lat), (east_lon, south_lat), (west_lon, south_lat)

    partners = (
        ((east_lon, lat), None),
        ((west_lon, lat), None),
        (north, None),
        (north_east, jnp.logical_not(east_is_self)),
        (north_west, jnp.logical_not(west_is_self)),
        (south, above_bottom),
        (south_east, above_bottom),
        (south_west, above_bottom),
    )

    def under(condition, action):
        if condition is None:
            action()
        else:
            pl.when(condition)(action)

    barrier = pltpu.get_barrier_semaphore()
    for device, condition in partners:
        under(
            condition,
            lambda device=device: pl.semaphore_signal(
                barrier, 1, device_id=device, device_id_type=MESH
            ),
        )

    loads = [
        pltpu.make_async_copy(source, target, load_sem.at[number])
        for number, (source, target) in enumerate(
            (
                (levels_hbm, levels.at[pl.ds(PAD, ROWS)]),
                (tracers_hbm, tracers_in),
                (east_hbm, east_in),
                (north_hbm, north_in),
                (kappa_hbm, kappa_in),
            )
        )
    ]
    for copy in loads:
        copy.start()

    @pl.when(at_bottom)
    def _():
        zero = jnp.zeros((LEVELS, COLS), jnp.float32)
        levels[pl.ds(0, PAD)] = jnp.zeros((PAD, COLS), jnp.int32)
        for row in range(PAD - REACH, PAD):
            for number in range(5):
                cells[row, number] = zero
        from_west[0] = zero
        from_east[0] = zero

    for copy in loads:
        copy.wait()

    depth = lax.broadcasted_iota(jnp.int32, (LEVELS, COLS), 0)

    def wet_row(row):
        return (depth < levels[pl.ds(row, 1)]).astype(jnp.float32)

    def gather(number):
        eastern = jnp.zeros((LEVELS, COLS), jnp.float32)
        western = jnp.zeros((LEVELS, COLS), jnp.float32)
        for group in range(GROUPS):
            row = number + STRIDE * group
            values = [
                tracers_in[pl.ds(row, LEVELS, stride=ROWS)],
                tracers_in[pl.ds(row + LEVELS * ROWS, LEVELS, stride=ROWS)],
                east_in[pl.ds(row, LEVELS, stride=ROWS)],
                north_in[pl.ds(row, LEVELS, stride=ROWS)],
                kappa_in[pl.ds(row, LEVELS, stride=ROWS)],
                wet_row(row + PAD),
            ]
            for which in range(5):
                cells[row + PAD, which] = values[which]
            wet[row + PAD] = values[WET]
            for which, (width, end) in enumerate(SLOTS):
                last = LANES * group + end
                inside = jnp.logical_and(lane >= last - width, lane < last)
                eastern = jnp.where(inside, roll(values[which], last), eastern)
                start = LANES * (group + 1) - end
                inside = jnp.logical_and(lane >= start, lane < start + width)
                western = jnp.where(inside, roll(values[which], start), western)
        to_east[number] = eastern
        to_west[number] = western

    def gather_pair(pair, carry):
        gather(2 * pair)
        gather(2 * pair + 1)
        return carry

    lax.fori_loop(0, STRIDE // 2, gather_pair, 0)

    for side, corner in ((to_east, corner_east), (to_west, corner_west)):
        for number, rows in enumerate((range(GROUPS), range(ROWS - GROUPS, ROWS))):
            packed = side[rows[0] % STRIDE]
            for row in rows:
                moved = roll(side[row % STRIDE], LANES * (row % GROUPS - row // STRIDE))
                packed = jnp.where(lane // LANES == row % GROUPS, moved, packed)
            corner[number] = packed

    count = 3 + sum(
        condition.astype(jnp.int32) for _, condition in partners if condition is not None
    )
    pl.semaphore_wait(barrier, count)

    own = pl.ds(1, STRIDE)
    low, high = pl.ds(0, 1), pl.ds(1 + STRIDE, 1)
    high_corner = pl.ds(1, 1)
    low_rows, high_rows = pl.ds(PAD - REACH, REACH), pl.ds(PAD + ROWS, REACH)
    first_rows, last_rows = pl.ds(PAD, REACH), pl.ds(PAD + ROWS - REACH, REACH)

    def remote(source, target, send, receive, device):
        return pltpu.make_async_remote_copy(
            src_ref=source,
            dst_ref=target,
            send_sem=send_sem.at[send],
            recv_sem=recv_sem.at[receive],
            device_id=device,
            device_id_type=MESH,
        )

    remote(to_east, from_west.at[own], 0, 0, (east_lon, lat)).start()
    remote(to_west, from_east.at[own], 1, 1, (west_lon, lat)).start()

    @pl.when(at_top)
    def _():
        remote(cells.at[last_rows], cells.at[high_rows], 6, 7, north).start()
        remote(levels.at[pl.ds(ROWS, 8)], levels.at[pl.ds(PAD + ROWS, 8)], 8, 9, north).start()

        @pl.when(jnp.logical_not(east_is_self))
        def _():
            remote(corner_east.at[high_corner], from_east.at[high], 2, 5, north_east).start()

        @pl.when(jnp.logical_not(west_is_self))
        def _():
            remote(corner_west.at[high_corner], from_west.at[high], 3, 4, north_west).start()

        @pl.when(east_is_self)
        def _():
            from_east[high] = corner_east[high_corner]

        @pl.when(west_is_self)
        def _():
            from_west[high] = corner_west[high_corner]

    @pl.when(below_top)
    def _():
        remote(corner_east.at[high_corner], from_west.at[low], 2, 2, north_east).start()
        remote(corner_west.at[high_corner], from_east.at[low], 3, 3, north_west).start()

    @pl.when(above_bottom)
    def _():
        remote(corner_east.at[low], from_west.at[high], 4, 4, south_east).start()
        remote(corner_west.at[low], from_east.at[high], 5, 5, south_west).start()

    def send_rows():
        @pl.when(above_bottom)
        def _():
            remote(levels.at[pl.ds(PAD, 8)], levels.at[pl.ds(PAD + ROWS, 8)], 9, 9, south).start()
            remote(cells.at[first_rows], cells.at[high_rows], 7, 7, south).start()

        @pl.when(below_top)
        def _():
            remote(levels.at[pl.ds(ROWS, 8)], levels.at[pl.ds(0, 8)], 8, 8, north).start()
            remote(cells.at[last_rows], cells.at[low_rows], 6, 6, north).start()

    send_rows()


    group_lane = lane % LANES
    left_halo, right_halo = group_lane < REACH, group_lane >= LANES - REACH
    to_left, to_right = REACH, LANES - REACH

    def edges(value, group):
        return jnp.where(
            lane < LANES * group + LANES // 2,
            roll(value, LANES * group + to_left),
            roll(value, LANES * group + to_right),
        )

    def packed_rows(read):
        total = edges(read(0), 0)
        for group in range(1, GROUPS):
            total = jnp.where(lane // LANES == group, edges(read(group), group), total)
        return total

    def strip_own(number, carry):
        for k in range(2):
            first = PAD + 2 * number + k
            target = REACH + 2 * number + k
            for which in range(5):
                strip[target, which] = packed_rows(
                    lambda group, which=which: cells[first + STRIDE * group, which]
                )
            strip[target, WET] = packed_rows(lambda group: wet[first + STRIDE * group])
        return carry

    lax.fori_loop(0, STRIDE // 2, strip_own, 0)

    main_parts = (
        lambda row: cells[row, EAST],
        lambda row: cells[row, NORTH],
        lambda row: cells[row, KAPPA],
        lambda row: wet[row],
    )
    strip_parts = tuple(
        lambda row, which=which: strip[row, which] for which in (EAST, NORTH, KAPPA, WET)
    )

    def main_coefficients(number, carry):
        for k in range(9):
            coefficients(PAD + 1 + 9 * number + k, *main_parts, main_coef)
        return carry

    lax.fori_loop(0, 5, main_coefficients, 0)

    def keep(target):
        def store(row, tracer, value):
            target[row, tracer] = value

        return store

    def reading(source):
        return lambda row, tracer: source[row, tracer]

    stages = (reading(cells), reading(main_1), reading(main_2))
    targets = (keep(main_1), keep(main_2), keep(main_3))
    for step, width in enumerate((11, 10, 12)):
        margin = 2 * (step + 1)
        advance(stages[step], main_coef, PAD + margin, ROWS - 2 * margin, targets[step], width)


    def arrival(slot, target):
        remote(target, target, slot, slot, (lon, lat)).wait_recv()

    def departure(slot, source):
        remote(source, source, slot, slot, (lon, lat)).wait_send()

    arrival(7, cells.at[high_rows])
    arrival(9, levels.at[pl.ds(PAD + ROWS, 8)])

    @pl.when(above_bottom)
    def _():
        arrival(6, cells.at[low_rows])
        arrival(8, levels.at[pl.ds(0, 8)])

    north_start = PAD + ROWS
    raw_start = jnp.where(at_top, north_start + 2, north_start)
    for k in range(REACH):
        wet[PAD - REACH + k] = wet_row(PAD - REACH + k)
        wet[north_start + k] = wet_row(raw_start + k)

    @pl.when(at_top)
    def _():
        def swap(k, carry):
            one, other = north_start + k, north_start + REACH - 1 - k
            for which in range(5):
                near, far = cells[one, which], cells[other, which]
                cells[one, which], cells[other, which] = reverse(far), reverse(near)
            near, far = wet[one], wet[other]
            wet[one], wet[other] = reverse(far), reverse(near)
            return carry

        lax.fori_loop(0, REACH // 2, swap, 0)

    def strip_ghost(k, carry):
        for which in range(6):
            def read(row, which=which):
                return wet[row] if which == WET else cells[row, which]

            strip[k, which] = edges(read(PAD - REACH + k), 0)
            strip[REACH + STRIDE + k, which] = edges(read(north_start + k), GROUPS - 1)
        return carry

    lax.fori_loop(0, REACH, strip_ghost, 0)

    top_speed[...] = cells[north_start - 1, NORTH]

    @pl.when(at_top)
    def _():
        top_speed[...] = 0.5 * (top_speed[...] - cells[north_start, NORTH])
        for k in range(4):
            row = north_start + k
            cells[row, NORTH] = -cells[row + 1, NORTH]
            cells[row, EAST] = -roll(cells[row, EAST], -1)

    for row in (3, 4, 5, 6, 7, 8, 54, 56, 57, 58, 59):
        coefficients(row, *main_parts, main_coef)
    coefficients(
        north_start - 1, main_parts[0], lambda row: top_speed[...], *main_parts[2:], main_coef
    )

    for step in range(3):
        reach = REACH - 2 * (step + 1)
        advance(stages[step], main_coef, PAD - reach, REACH, targets[step], REACH)
        advance(stages[step], main_coef, PAD + ROWS - 2 * (step + 1), REACH, targets[step], REACH)

    def inner(k, carry):
        for tracer in range(2):
            near = packed_rows(lambda group: main_1[PAD + k + STRIDE * group, tracer])
            strip_in[REACH + k, tracer] = near
        return carry

    lax.fori_loop(0, STRIDE, inner, 0)
    for k in range(4):
        for tracer in range(2):
            strip_in[2 + k, tracer] = jnp.where(
                lane < LANES,
                edges(main_1[PAD - 4 + k, tracer], 0),
                roll(strip_in[STRIDE + 2 + k, tracer], LANES),
            )
            strip_in[REACH + STRIDE + k, tracer] = jnp.where(
                lane >= COLS - LANES,
                edges(main_1[north_start + k, tracer], GROUPS - 1),
                roll(strip_in[REACH + k, tracer], -LANES),
            )

    @pl.when(above_bottom)
    def _():
        arrival(2, from_west.at[low])
        arrival(3, from_east.at[low])

    pl.when(jnp.logical_not(west_is_self))(lambda: arrival(4, from_west.at[high]))
    pl.when(jnp.logical_not(east_is_self))(lambda: arrival(5, from_east.at[high]))

    @pl.when(at_top)
    def _():
        for side in (from_west, from_east):
            side[1 + STRIDE] = reverse(side[1 + STRIDE])

    arrival(0, from_west.at[own])
    arrival(1, from_east.at[own])

    def halo(number, shift, which):
        end = SLOTS[which][1]
        return jnp.where(
            left_halo,
            roll(from_west[number], shift + REACH - end),
            roll(from_east[number], shift + end - REACH),
        )

    outside = jnp.logical_or(left_halo, right_halo)

    def strip_edges(number, carry):
        for k in range(6):
            place = 6 * number + k
            for which in range(6):
                strip[REACH + place, which] = jnp.where(
                    outside, halo(1 + place, 0, which), strip[REACH + place, which]
                )
        return carry

    lax.fori_loop(0, STRIDE // 6, strip_edges, 0)

    for k in range(REACH):
        place = REACH + STRIDE + k
        for which in range(6):
            lowest, highest = strip[k, which], strip[place, which]
            if k >= REACH - GROUPS:
                corner = halo(0, -LANES * (k - REACH + GROUPS), which)
                lowest = jnp.where(outside, corner, lowest)
            if k < GROUPS:
                corner = halo(1 + STRIDE, LANES * (GROUPS - 1 - k), which)
                highest = jnp.where(outside, corner, highest)
            strip[k, which] = jnp.where(lane < LANES, lowest, roll(strip[STRIDE + k, which], LANES))
            strip[place, which] = jnp.where(
                lane >= COLS - LANES, highest, roll(strip[REACH + k, which], -LANES)
            )

    @pl.when(at_top)
    def _():
        top_group = lane >= COLS - LANES
        last = REACH + STRIDE - 1
        north = strip[last, NORTH]
        strip[last, NORTH] = jnp.where(top_group, 0.5 * (north - strip[last + 1, NORTH]), north)
        for place in range(last + 1, last + 5):
            north, east = strip[place, NORTH], strip[place, EAST]
            strip[place, NORTH] = jnp.where(top_group, -strip[place + 1, NORTH], north)
            strip[place, EAST] = jnp.where(top_group, -roll(east, -1), east)

    for place in range(1, STRIPS - 2):
        coefficients(place, *strip_parts, strip_coef)

    lost = jnp.logical_and(group_lane >= LANES // 2 - 2, group_lane < LANES // 2 + 2)

    def first_store(place, tracer, value):
        strip_1[place, tracer] = jnp.where(lost, strip_in[place, tracer], value)

    def finish(place, tracer, value):
        for group in range(GROUPS):
            row = place - REACH + STRIDE * group
            merged = jnp.where(
                lane < REACH,
                roll(value, -LANES * group - to_left),
                jnp.where(
                    lane >= COLS - REACH,
                    roll(value, -LANES * group - to_right),
                    main_3[row + PAD, tracer],
                ),
            )
            out_ref[pl.ds(tracer * LEVELS * ROWS + row, LEVELS, stride=ROWS)] = merged

    advance(reading(strip), strip_coef, 2, STRIPS - 4, first_store, 10)
    advance(reading(strip_1), strip_coef, 4, STRIPS - 8, keep(strip_2), 8)
    advance(reading(strip_2), strip_coef, REACH, STRIDE, finish, 6)

    departure(0, to_east)
    departure(1, to_west)
    pl.when(jnp.logical_not(east_is_self))(lambda: departure(2, corner_east.at[high_corner]))
    pl.when(jnp.logical_not(west_is_self))(lambda: departure(3, corner_west.at[high_corner]))
    departure(6, cells.at[last_rows])
    departure(8, levels.at[pl.ds(ROWS, 8)])

    @pl.when(above_bottom)
    def _():
        departure(4, corner_east.at[low])
        departure(5, corner_west.at[low])
        departure(7, cells.at[first_rows])
        departure(9, levels.at[pl.ds(PAD, 8)])


def per_device(nlon, nlat, tracers, east_courant, north_courant, diffusivity, wet_levels):
    flat = LEVELS * ROWS
    f32 = jnp.float32
    vreg = (LEVELS, COLS)
    result = pl.pallas_call(
        functools.partial(kernel, nlon, nlat),
        out_shape=pltpu.VMEM((2 * flat, COLS), f32),
        in_specs=[pl.BlockSpec(memory_space=pl.ANY)] * 5,
        out_specs=pl.BlockSpec(memory_space=pltpu.VMEM),
        scratch_shapes=[
            pltpu.VMEM((2 * flat, COLS), f32),
            pltpu.VMEM((flat, COLS), f32),
            pltpu.VMEM((flat, COLS), f32),
            pltpu.VMEM((flat, COLS), f32),
            pltpu.VMEM((SPAN, COLS), jnp.int32),
            pltpu.VMEM((SPAN, 5) + vreg, f32),
            pltpu.VMEM((SPAN,) + vreg, f32),
            pltpu.VMEM((STRIDE,) + vreg, f32),
            pltpu.VMEM((STRIDE,) + vreg, f32),
            pltpu.VMEM((2,) + vreg, f32),
            pltpu.VMEM((2,) + vreg, f32),
            pltpu.VMEM((STRIDE + 2,) + vreg, f32),
            pltpu.VMEM((STRIDE + 2,) + vreg, f32),
            pltpu.VMEM((STRIPS, 6) + vreg, f32),
            pltpu.VMEM((SPAN, 6) + vreg, f32),
            pltpu.VMEM((STRIPS, 6) + vreg, f32),
            pltpu.VMEM((SPAN, 2) + vreg, f32),
            pltpu.VMEM((SPAN, 2) + vreg, f32),
            pltpu.VMEM((SPAN, 2) + vreg, f32),
            pltpu.VMEM((STRIPS, 2) + vreg, f32),
            pltpu.VMEM((STRIPS, 2) + vreg, f32),
            pltpu.VMEM((STRIPS, 2) + vreg, f32),
            pltpu.VMEM(vreg, f32),
            pltpu.SemaphoreType.DMA((5,)),
            pltpu.SemaphoreType.DMA((10,)),
            pltpu.SemaphoreType.DMA((10,)),
        ],
        compiler_params=pltpu.CompilerParams(
            collective_id=0, has_side_effects=True, vmem_limit_bytes=56 << 20
        ),
        name="advect",
    )(
        tracers.reshape(2 * flat, COLS),
        east_courant.reshape(flat, COLS),
        north_courant.reshape(flat, COLS),
        diffusivity.reshape(flat, COLS),
        wet_levels,
    )
    return result.reshape(2, LEVELS, ROWS, COLS)


def solution(mesh):
    placed = (
        P(None, None, "lat", "lon"),
        P(None, "lat", "lon"),
        P(None, "lat", "lon"),
        P(None, "lat", "lon"),
        P("lat", "lon"),
    )
    return jax.shard_map(
        functools.partial(per_device, mesh.shape["lon"], mesh.shape["lat"]),
        mesh=mesh,
        in_specs=placed,
        out_specs=P(None, None, "lat", "lon"),
        check_vma=False,
    )
```

```python
import functools

import jax
import jax.numpy as jnp
from jax import lax
from jax.experimental import pallas as pl
from jax.experimental.pallas import tpu as pltpu
from jax.sharding import PartitionSpec as P

MESH = pl.DeviceIdType.MESH
LEVELS, ROWS, COLS = 8, 48, 128
PAD = 8
SPAN = ROWS + 2 * PAD
REACH = 6
GROUPS, LANES = 4, 32
STRIDE = ROWS // GROUPS
STRIPS = STRIDE + 2 * REACH
T0, T1, EAST, NORTH, KAPPA, WET = range(6)
SLOTS = ((6, 6), (6, 12), (5, 17), (4, 21), (5, 26), (5, 31))


def roll(value, shift):
    return pltpu.roll(value, shift % COLS, 1)


def lane_index():
    return lax.broadcasted_iota(jnp.int32, (LEVELS, COLS), 1)


def reverse(value):
    return jnp.take_along_axis(value, COLS - 1 - lane_index(), axis=1, mode="promise_in_bounds")


def face(speed, kappa_sum, mask):
    speed = speed * mask
    magnitude = jnp.abs(speed)
    return (
        speed,
        jnp.minimum(speed, 0.0) - 0.5 * kappa_sum * mask,
        0.5 * magnitude * (1.0 - magnitude),
    )


def flux(cell, before, here, after, coef):
    speed, drift, limit = coef
    upslope = jnp.where(speed > 0, before, after)
    limited = jnp.minimum(jnp.maximum(upslope, jnp.minimum(here, 0.0)), jnp.maximum(here, 0.0))
    return speed * cell + drift * here + limit * limited


def coefficients(row, east, north, kappa, wet, out):
    here, above = kappa(row), kappa(row + 1)
    wet_here, wet_above = wet(row), wet(row + 1)
    along = face(east(row), here + roll(here, -1), wet_here * roll(wet_here, -1))
    across = face(north(row), here + above, wet_here * wet_above)
    for number, value in enumerate(along + across):
        out[row, number] = value


def advance(source, coef, start, count, store, width):
    def north_flux(row, tracer, cell, diffs):
        return flux(cell, *diffs, tuple(coef[row, 3 + k] for k in range(3)))

    def first_flux(tracer):
        cells = [source(start - 2 + k, tracer) for k in range(4)]
        diffs = [cells[k + 1] - cells[k] for k in range(3)]
        return north_flux(start - 1, tracer, cells[1], diffs)

    def body(number, below):
        base = start + number * width
        below = list(below)
        for tracer in range(2):
            cells = [source(base - 1 + k, tracer) for k in range(width + 3)]
            diffs = [cells[k + 1] - cells[k] for k in range(width + 2)]
            for k in range(width):
                row = base + k
                cell = cells[k + 1]
                here = roll(cell, -1) - cell
                along = flux(
                    cell, roll(here, 1), here, roll(here, -1), tuple(coef[row, i] for i in range(3))
                )
                across = north_flux(row, tracer, cell, diffs[k : k + 3])
                store(row, tracer, cell - (along - roll(along, 1)) - (across - below[tracer]))
                below[tracer] = across
        return tuple(below)

    below = (first_flux(0), first_flux(1))
    if count == width:
        body(0, below)
    else:
        lax.fori_loop(0, count // width, body, below)


def kernel(
    nlon, nlat,
    tracers_hbm, east_hbm, north_hbm, kappa_hbm, levels_hbm, out_ref,
    tracers_in, east_in, north_in, kappa_in, levels,
    cells, wet, to_east, to_west, corner_east, corner_west, from_west, from_east, strip,
    main_coef, strip_coef, main_1, main_2, main_3, strip_in, strip_1, strip_2, top_speed,
    load_sem, send_sem, recv_sem,
):
    lon, lat = lax.axis_index("lon"), lax.axis_index("lat")
    at_top, at_bottom = lat == nlat - 1, lat == 0
    below_top, above_bottom = jnp.logical_not(at_top), jnp.logical_not(at_bottom)
    east_lon, west_lon = lax.rem(lon + 1, nlon), lax.rem(lon + nlon - 1, nlon)
    fold_lon, fold_east, fold_west = nlon - 1 - lon, nlon - 1 - east_lon, nlon - 1 - west_lon
    east_is_self = jnp.logical_and(at_top, fold_east == lon)
    west_is_self = jnp.logical_and(at_top, fold_west == lon)
    lane = lane_index()

    north_lat = jnp.where(at_top, lat, lat + 1)
    south_lat = jnp.where(at_bottom, lat, lat - 1)
    north = (jnp.where(at_top, fold_lon, lon), north_lat)
    north_east = (jnp.where(at_top, fold_east, east_lon), north_lat)
    north_west = (jnp.where(at_top, fold_west, west_lon), north_lat)
    south, south_east, south_west = (lon, south_lat), (east_lon, south_lat), (west_lon, south_lat)

    partners = (
        ((east_lon, lat), None),
        ((west_lon, lat), None),
        (north, None),
        (north_east, jnp.logical_not(east_is_self)),
        (north_west, jnp.logical_not(west_is_self)),
        (south, above_bottom),
        (south_east, above_bottom),
        (south_west, above_bottom),
    )

    def under(condition, action):
        if condition is None:
            action()
        else:
            pl.when(condition)(action)

    barrier = pltpu.get_barrier_semaphore()
    for device, condition in partners:
        under(
            condition,
            lambda device=device: pl.semaphore_signal(
                barrier, 1, device_id=device, device_id_type=MESH
            ),
        )

    loads = [
        pltpu.make_async_copy(source, target, load_sem.at[number])
        for number, (source, target) in enumerate(
            (
                (levels_hbm, levels.at[pl.ds(PAD, ROWS)]),
                (tracers_hbm, tracers_in),
                (east_hbm, east_in),
                (north_hbm, north_in),
                (kappa_hbm, kappa_in),
            )
        )
    ]
    for copy in loads:
        copy.start()

    @pl.when(at_bottom)
    def _():
        zero = jnp.zeros((LEVELS, COLS), jnp.float32)
        levels[pl.ds(0, PAD)] = jnp.zeros((PAD, COLS), jnp.int32)
        for row in range(PAD - REACH, PAD):
            for number in range(5):
                cells[row, number] = zero
        from_west[0] = zero
        from_east[0] = zero

    for copy in loads:
        copy.wait()

    depth = lax.broadcasted_iota(jnp.int32, (LEVELS, COLS), 0)

    def wet_row(row):
        return (depth < levels[pl.ds(row, 1)]).astype(jnp.float32)

    def gather(number):
        eastern = jnp.zeros((LEVELS, COLS), jnp.float32)
        western = jnp.zeros((LEVELS, COLS), jnp.float32)
        for group in range(GROUPS):
            row = number + STRIDE * group
            values = [
                tracers_in[pl.ds(row, LEVELS, stride=ROWS)],
                tracers_in[pl.ds(row + LEVELS * ROWS, LEVELS, stride=ROWS)],
                east_in[pl.ds(row, LEVELS, stride=ROWS)],
                north_in[pl.ds(row, LEVELS, stride=ROWS)],
                kappa_in[pl.ds(row, LEVELS, stride=ROWS)],
                wet_row(row + PAD),
            ]
            for which in range(5):
                cells[row + PAD, which] = values[which]
            wet[row + PAD] = values[WET]
            for which, (width, end) in enumerate(SLOTS):
                last = LANES * group + end
                inside = jnp.logical_and(lane >= last - width, lane < last)
                eastern = jnp.where(inside, roll(values[which], last), eastern)
                start = LANES * (group + 1) - end
                inside = jnp.logical_and(lane >= start, lane < start + width)
                western = jnp.where(inside, roll(values[which], start), western)
        to_east[number] = eastern
        to_west[number] = western

    def gather_pair(pair, carry):
        gather(2 * pair)
        gather(2 * pair + 1)
        return carry

    lax.fori_loop(0, STRIDE // 2, gather_pair, 0)

    for side, corner in ((to_east, corner_east), (to_west, corner_west)):
        for number, rows in enumerate((range(GROUPS), range(ROWS - GROUPS, ROWS))):
            packed = side[rows[0] % STRIDE]
            for row in rows:
                moved = roll(side[row % STRIDE], LANES * (row % GROUPS - row // STRIDE))
                packed = jnp.where(lane // LANES == row % GROUPS, moved, packed)
            corner[number] = packed

    count = 3 + sum(
        condition.astype(jnp.int32) for _, condition in partners if condition is not None
    )
    pl.semaphore_wait(barrier, count)

    own = pl.ds(1, STRIDE)
    low, high = pl.ds(0, 1), pl.ds(1 + STRIDE, 1)
    high_corner = pl.ds(1, 1)
    inner_count, both = REACH - 1, pl.ds(0, 2)

    def part(inner, outer):
        return cells.at[pl.ds(inner, inner_count)], cells.at[pl.ds(outer, 1), both]

    first_rows = part(PAD, PAD + inner_count)
    last_rows = part(PAD + ROWS - inner_count, PAD + ROWS - REACH)
    low_rows = part(PAD - inner_count, PAD - REACH)
    high_rows = part(PAD + ROWS, PAD + ROWS + inner_count)
    fold_rows = part(PAD + ROWS + 1, PAD + ROWS)

    def remote(source, target, send, receive, device):
        return pltpu.make_async_remote_copy(
            src_ref=source,
            dst_ref=target,
            send_sem=send_sem.at[send],
            recv_sem=recv_sem.at[receive],
            device_id=device,
            device_id_type=MESH,
        )

    remote(to_east, from_west.at[own], 0, 0, (east_lon, lat)).start()
    remote(to_west, from_east.at[own], 1, 1, (west_lon, lat)).start()

    @pl.when(at_top)
    def _():
        for k in range(2):
            remote(last_rows[k], fold_rows[k], 6 + 4 * k, 7 + 4 * k, north).start()
        remote(levels.at[pl.ds(ROWS, 8)], levels.at[pl.ds(PAD + ROWS, 8)], 8, 9, north).start()

        @pl.when(jnp.logical_not(east_is_self))
        def _():
            remote(corner_east.at[high_corner], from_east.at[high], 2, 5, north_east).start()

        @pl.when(jnp.logical_not(west_is_self))
        def _():
            remote(corner_west.at[high_corner], from_west.at[high], 3, 4, north_west).start()

        @pl.when(east_is_self)
        def _():
            from_east[high] = corner_east[high_corner]

        @pl.when(west_is_self)
        def _():
            from_west[high] = corner_west[high_corner]

    @pl.when(below_top)
    def _():
        remote(corner_east.at[high_corner], from_west.at[low], 2, 2, north_east).start()
        remote(corner_west.at[high_corner], from_east.at[low], 3, 3, north_west).start()

    @pl.when(above_bottom)
    def _():
        remote(corner_east.at[low], from_west.at[high], 4, 4, south_east).start()
        remote(corner_west.at[low], from_east.at[high], 5, 5, south_west).start()

    def send_rows():
        @pl.when(above_bottom)
        def _():
            remote(levels.at[pl.ds(PAD, 8)], levels.at[pl.ds(PAD + ROWS, 8)], 9, 9, south).start()
            for k in range(2):
                remote(first_rows[k], high_rows[k], 7 + 4 * k, 7 + 4 * k, south).start()

        @pl.when(below_top)
        def _():
            remote(levels.at[pl.ds(ROWS, 8)], levels.at[pl.ds(0, 8)], 8, 8, north).start()
            for k in range(2):
                remote(last_rows[k], low_rows[k], 6 + 4 * k, 6 + 4 * k, north).start()

    send_rows()


    group_lane = lane % LANES
    left_halo, right_halo = group_lane < REACH, group_lane >= LANES - REACH
    to_left, to_right = REACH, LANES - REACH

    def edges(value, group):
        return jnp.where(
            lane < LANES * group + LANES // 2,
            roll(value, LANES * group + to_left),
            roll(value, LANES * group + to_right),
        )

    def packed_rows(read):
        total = edges(read(0), 0)
        for group in range(1, GROUPS):
            total = jnp.where(lane // LANES == group, edges(read(group), group), total)
        return total

    def strip_own(number, carry):
        for k in range(2):
            first = PAD + 2 * number + k
            target = REACH + 2 * number + k
            for which in range(5):
                strip[target, which] = packed_rows(
                    lambda group, which=which: cells[first + STRIDE * group, which]
                )
            strip[target, WET] = packed_rows(lambda group: wet[first + STRIDE * group])
        return carry

    lax.fori_loop(0, STRIDE // 2, strip_own, 0)

    main_parts = (
        lambda row: cells[row, EAST],
        lambda row: cells[row, NORTH],
        lambda row: cells[row, KAPPA],
        lambda row: wet[row],
    )
    strip_parts = tuple(
        lambda row, which=which: strip[row, which] for which in (EAST, NORTH, KAPPA, WET)
    )

    def main_coefficients(number, carry):
        for k in range(9):
            coefficients(PAD + 1 + 9 * number + k, *main_parts, main_coef)
        return carry

    lax.fori_loop(0, 5, main_coefficients, 0)

    def keep(target):
        def store(row, tracer, value):
            target[row, tracer] = value

        return store

    def reading(source):
        return lambda row, tracer: source[row, tracer]

    stages = (reading(cells), reading(main_1), reading(main_2))
    targets = (keep(main_1), keep(main_2), keep(main_3))
    for step, width in enumerate((11, 10, 12)):
        margin = 2 * (step + 1)
        advance(stages[step], main_coef, PAD + margin, ROWS - 2 * margin, targets[step], width)


    def arrival(slot, target):
        remote(target, target, slot, slot, (lon, lat)).wait_recv()

    def departure(slot, source):
        remote(source, source, slot, slot, (lon, lat)).wait_send()

    @pl.when(at_top)
    def _():
        for k in range(2):
            arrival(7 + 4 * k, fold_rows[k])

    @pl.when(below_top)
    def _():
        for k in range(2):
            arrival(7 + 4 * k, high_rows[k])

    arrival(9, levels.at[pl.ds(PAD + ROWS, 8)])

    @pl.when(above_bottom)
    def _():
        for k in range(2):
            arrival(6 + 4 * k, low_rows[k])
        arrival(8, levels.at[pl.ds(0, 8)])

    north_start = PAD + ROWS
    raw_start = jnp.where(at_top, north_start + 2, north_start)
    for k in range(REACH):
        wet[PAD - REACH + k] = wet_row(PAD - REACH + k)
        wet[north_start + k] = wet_row(raw_start + k)

    @pl.when(at_top)
    def _():
        def swap(k, carry):
            one, other = north_start + k, north_start + REACH - 1 - k
            for which in range(5):
                near, far = cells[one, which], cells[other, which]
                cells[one, which], cells[other, which] = reverse(far), reverse(near)
            near, far = wet[one], wet[other]
            wet[one], wet[other] = reverse(far), reverse(near)
            return carry

        lax.fori_loop(0, REACH // 2, swap, 0)

    def strip_ghost(k, carry):
        for which in range(6):
            def read(row, which=which):
                return wet[row] if which == WET else cells[row, which]

            strip[k, which] = edges(read(PAD - REACH + k), 0)
            strip[REACH + STRIDE + k, which] = edges(read(north_start + k), GROUPS - 1)
        return carry

    lax.fori_loop(0, REACH, strip_ghost, 0)

    top_speed[...] = cells[north_start - 1, NORTH]

    @pl.when(at_top)
    def _():
        top_speed[...] = 0.5 * (top_speed[...] - cells[north_start, NORTH])
        for k in range(4):
            row = north_start + k
            cells[row, NORTH] = -cells[row + 1, NORTH]
            cells[row, EAST] = -roll(cells[row, EAST], -1)

    for row in (3, 4, 5, 6, 7, 8, 54, 56, 57, 58, 59):
        coefficients(row, *main_parts, main_coef)
    coefficients(
        north_start - 1, main_parts[0], lambda row: top_speed[...], *main_parts[2:], main_coef
    )

    for step in range(3):
        reach = REACH - 2 * (step + 1)
        advance(stages[step], main_coef, PAD - reach, REACH, targets[step], REACH)
        advance(stages[step], main_coef, PAD + ROWS - 2 * (step + 1), REACH, targets[step], REACH)

    def inner(k, carry):
        for tracer in range(2):
            near = packed_rows(lambda group: main_1[PAD + k + STRIDE * group, tracer])
            strip_in[REACH + k, tracer] = near
        return carry

    lax.fori_loop(0, STRIDE, inner, 0)
    for k in range(4):
        for tracer in range(2):
            strip_in[2 + k, tracer] = jnp.where(
                lane < LANES,
                edges(main_1[PAD - 4 + k, tracer], 0),
                roll(strip_in[STRIDE + 2 + k, tracer], LANES),
            )
            strip_in[REACH + STRIDE + k, tracer] = jnp.where(
                lane >= COLS - LANES,
                edges(main_1[north_start + k, tracer], GROUPS - 1),
                roll(strip_in[REACH + k, tracer], -LANES),
            )

    @pl.when(above_bottom)
    def _():
        arrival(2, from_west.at[low])
        arrival(3, from_east.at[low])

    pl.when(jnp.logical_not(west_is_self))(lambda: arrival(4, from_west.at[high]))
    pl.when(jnp.logical_not(east_is_self))(lambda: arrival(5, from_east.at[high]))

    @pl.when(at_top)
    def _():
        for side in (from_west, from_east):
            side[1 + STRIDE] = reverse(side[1 + STRIDE])

    arrival(0, from_west.at[own])
    arrival(1, from_east.at[own])

    def halo(number, shift, which):
        end = SLOTS[which][1]
        return jnp.where(
            left_halo,
            roll(from_west[number], shift + REACH - end),
            roll(from_east[number], shift + end - REACH),
        )

    outside = jnp.logical_or(left_halo, right_halo)

    def strip_edges(number, carry):
        for k in range(6):
            place = 6 * number + k
            for which in range(6):
                strip[REACH + place, which] = jnp.where(
                    outside, halo(1 + place, 0, which), strip[REACH + place, which]
                )
        return carry

    lax.fori_loop(0, STRIDE // 6, strip_edges, 0)

    for k in range(REACH):
        place = REACH + STRIDE + k
        for which in range(6):
            lowest, highest = strip[k, which], strip[place, which]
            if k >= REACH - GROUPS:
                corner = halo(0, -LANES * (k - REACH + GROUPS), which)
                lowest = jnp.where(outside, corner, lowest)
            if k < GROUPS:
                corner = halo(1 + STRIDE, LANES * (GROUPS - 1 - k), which)
                highest = jnp.where(outside, corner, highest)
            strip[k, which] = jnp.where(lane < LANES, lowest, roll(strip[STRIDE + k, which], LANES))
            strip[place, which] = jnp.where(
                lane >= COLS - LANES, highest, roll(strip[REACH + k, which], -LANES)
            )

    @pl.when(at_top)
    def _():
        top_group = lane >= COLS - LANES
        last = REACH + STRIDE - 1
        north = strip[last, NORTH]
        strip[last, NORTH] = jnp.where(top_group, 0.5 * (north - strip[last + 1, NORTH]), north)
        for place in range(last + 1, last + 5):
            north, east = strip[place, NORTH], strip[place, EAST]
            strip[place, NORTH] = jnp.where(top_group, -strip[place + 1, NORTH], north)
            strip[place, EAST] = jnp.where(top_group, -roll(east, -1), east)

    for place in range(1, STRIPS - 2):
        coefficients(place, *strip_parts, strip_coef)

    lost = jnp.logical_and(group_lane >= LANES // 2 - 2, group_lane < LANES // 2 + 2)

    def first_store(place, tracer, value):
        strip_1[place, tracer] = jnp.where(lost, strip_in[place, tracer], value)

    def finish(place, tracer, value):
        for group in range(GROUPS):
            row = place - REACH + STRIDE * group
            merged = jnp.where(
                lane < REACH,
                roll(value, -LANES * group - to_left),
                jnp.where(
                    lane >= COLS - REACH,
                    roll(value, -LANES * group - to_right),
                    main_3[row + PAD, tracer],
                ),
            )
            out_ref[pl.ds(tracer * LEVELS * ROWS + row, LEVELS, stride=ROWS)] = merged

    advance(reading(strip), strip_coef, 2, STRIPS - 4, first_store, 10)
    advance(reading(strip_1), strip_coef, 4, STRIPS - 8, keep(strip_2), 8)
    advance(reading(strip_2), strip_coef, REACH, STRIDE, finish, 6)

    departure(0, to_east)
    departure(1, to_west)
    pl.when(jnp.logical_not(east_is_self))(lambda: departure(2, corner_east.at[high_corner]))
    pl.when(jnp.logical_not(west_is_self))(lambda: departure(3, corner_west.at[high_corner]))
    for k in range(2):
        departure(6 + 4 * k, last_rows[k])
    departure(8, levels.at[pl.ds(ROWS, 8)])

    @pl.when(above_bottom)
    def _():
        departure(4, corner_east.at[low])
        departure(5, corner_west.at[low])
        for k in range(2):
            departure(7 + 4 * k, first_rows[k])
        departure(9, levels.at[pl.ds(PAD, 8)])


def per_device(nlon, nlat, tracers, east_courant, north_courant, diffusivity, wet_levels):
    flat = LEVELS * ROWS
    f32 = jnp.float32
    vreg = (LEVELS, COLS)
    result = pl.pallas_call(
        functools.partial(kernel, nlon, nlat),
        out_shape=pltpu.VMEM((2 * flat, COLS), f32),
        in_specs=[pl.BlockSpec(memory_space=pl.ANY)] * 5,
        out_specs=pl.BlockSpec(memory_space=pltpu.VMEM),
        scratch_shapes=[
            pltpu.VMEM((2 * flat, COLS), f32),
            pltpu.VMEM((flat, COLS), f32),
            pltpu.VMEM((flat, COLS), f32),
            pltpu.VMEM((flat, COLS), f32),
            pltpu.VMEM((SPAN, COLS), jnp.int32),
            pltpu.VMEM((SPAN, 5) + vreg, f32),
            pltpu.VMEM((SPAN,) + vreg, f32),
            pltpu.VMEM((STRIDE,) + vreg, f32),
            pltpu.VMEM((STRIDE,) + vreg, f32),
            pltpu.VMEM((2,) + vreg, f32),
            pltpu.VMEM((2,) + vreg, f32),
            pltpu.VMEM((STRIDE + 2,) + vreg, f32),
            pltpu.VMEM((STRIDE + 2,) + vreg, f32),
            pltpu.VMEM((STRIPS, 6) + vreg, f32),
            pltpu.VMEM((SPAN, 6) + vreg, f32),
            pltpu.VMEM((STRIPS, 6) + vreg, f32),
            pltpu.VMEM((SPAN, 2) + vreg, f32),
            pltpu.VMEM((SPAN, 2) + vreg, f32),
            pltpu.VMEM((SPAN, 2) + vreg, f32),
            pltpu.VMEM((STRIPS, 2) + vreg, f32),
            pltpu.VMEM((STRIPS, 2) + vreg, f32),
            pltpu.VMEM((STRIPS, 2) + vreg, f32),
            pltpu.VMEM(vreg, f32),
            pltpu.SemaphoreType.DMA((5,)),
            pltpu.SemaphoreType.DMA((12,)),
            pltpu.SemaphoreType.DMA((12,)),
        ],
        compiler_params=pltpu.CompilerParams(
            collective_id=0, has_side_effects=True, vmem_limit_bytes=56 << 20
        ),
        name="advect",
    )(
        tracers.reshape(2 * flat, COLS),
        east_courant.reshape(flat, COLS),
        north_courant.reshape(flat, COLS),
        diffusivity.reshape(flat, COLS),
        wet_levels,
    )
    return result.reshape(2, LEVELS, ROWS, COLS)


def solution(mesh):
    placed = (
        P(None, None, "lat", "lon"),
        P(None, "lat", "lon"),
        P(None, "lat", "lon"),
        P(None, "lat", "lon"),
        P("lat", "lon"),
    )
    return jax.shard_map(
        functools.partial(per_device, mesh.shape["lon"], mesh.shape["lat"]),
        mesh=mesh,
        in_specs=placed,
        out_specs=P(None, None, "lat", "lon"),
        check_vma=False,
    )
```
